32 devices in a mesh: dp: 8 (over y, x, core), seq: 4 (over z).
Axes of the slice: x: 2, y: 2, z: 4, core: 2. Of those that a mesh axis runs over, the one named last changes fastest.
Arguments:
- tokens: bfloat16 [8192, 2048], P(('dp', 'seq')), may hold values from -6 to 6
- queries: bfloat16 [8192, 1024], P(('dp', 'seq')), may hold values from -6 to 6
- kv_weight: bfloat16 [2048, 2048], P('seq'), may hold values from -0.0625 to 0.0625
- out_grad: bfloat16 [8192, 1024], P(('dp', 'seq')), may hold values from -6 to 6
Outputs:
- output: bfloat16 [8192, 1024], P(('dp', 'seq'))
- token_grad: bfloat16 [8192, 2048], P(('dp', 'seq'))
- query_grad: bfloat16 [8192, 1024], P(('dp', 'seq'))
- weight_grad: float32 [2048, 2048], P(('dp', 'seq'))
The draws below stay inside these ranges and needn't reach their ends.
All inputs are finite; a program needn't handle non-finite values.
Results may differ from the reference program's by a relative error of at most 0.014.
Values may be sent and summed in bfloat16 or wider, within the bound.
A program may use at most 128 MiB of HBM per device.

```python
import math
import jax
import jax.numpy as jnp
from jax import lax

D = 2048
HEADS = 8
HD = 128
TOK_DEV = 256
HW = 1024
LENGTH = 1024
TOKENS = 8192


def draw_kv_weight(key, part):
    first_key = jax.random.fold_in(key, 11)
    second_key = jax.random.fold_in(key, 12)
    columns = 2 * HEADS * HD
    entries = jax.random.truncated_normal(first_key, -4.0, 4.0, (D, columns), jnp.float32)
    column_scale = jnp.exp(jax.random.uniform(second_key, (columns,), jnp.float32, math.log(0.3), math.log(3.0)))
    limit = 0.0625
    values = jnp.clip(entries * column_scale[None, :] * (1.0 / math.sqrt(D)), -limit, limit)
    return values.astype(jnp.bfloat16)


def with_spikes(result, own_key, source, target, blocks, factor):
    def block_of(dim):
        return (jnp.arange(result.shape[dim]) // (result.shape[dim] // blocks)).reshape((-1,) + (1,) * (result.ndim - 1 - dim))

    first = jax.random.permutation(own_key, blocks)[block_of(target)]
    other_side = (block_of(target) + blocks // 2) % blocks
    return jnp.where((block_of(source) == first) | (block_of(source) == other_side), factor * result, result)


def level_of(own_key, dims, cuts, least, largest):
    level, own = 1.0, jax.random.fold_in(own_key, 6)
    for position, shards_of in cuts:
        draws = jnp.exp(jax.random.uniform(jax.random.fold_in(own, position), (shards_of,), jnp.float32, least / len(cuts), largest / len(cuts)))
        level = level * jnp.repeat(draws, dims[position] // shards_of).reshape([-1 if axis == position else 1 for axis in range(len(dims))])
    return level


def bell_draw(key, extent, width, most, pieces=(), dtype=jnp.bfloat16):
    level = level_of(key, extent, pieces, -0.22, 0.18) if pieces else 1.0
    result = jax.random.normal(key, extent, jnp.float32) * width * level
    return jnp.minimum(jnp.maximum(result, -most), most).astype(dtype)


def bell_draw_with(key, extent, scale, reach, pieces, heavy, dtype=jnp.bfloat16):
    values = scale * jax.random.normal(key, extent, jnp.float32)
    if pieces:
        values = values * level_of(key, extent, pieces, -0.22, 0.18)
    return jnp.clip(with_spikes(values, jax.random.fold_in(key, 3), *heavy), -reach, reach).astype(dtype)


def setup_inputs(seed: int = 0) -> dict:
    arg_keys = jax.random.split(jax.random.key(seed), 5)
    tokens = bell_draw_with(arg_keys[0], (TOKENS, D), 1.0, 6.0, ((0, 32),), (0, 1, 32, 2.75))
    queries = bell_draw(arg_keys[1], (TOKENS, HW), 1.0, 6.0, ((0, 32),))
    kv_weight = draw_kv_weight(jax.random.fold_in(arg_keys[4], 71), 0)
    out_grad = bell_draw(arg_keys[3], (TOKENS, HW), 1.0, 6.0, ((0, 32),))
    return {"tokens": tokens, "queries": queries, "kv_weight": kv_weight, "out_grad": out_grad}


epsilon = 1e-05

def feature(inputs):
    return jnp.where(inputs > 0, inputs + 1.0, jnp.exp(jnp.minimum(inputs, 0.0)))

def feature_slope(inputs):
    return jnp.where(inputs > 0, 1.0, jnp.exp(jnp.minimum(inputs, 0.0)))

def contract(formula, first_op, second_op):
    return jnp.einsum(formula, first_op, second_op, precision=lax.Precision.HIGHEST)

def reference(tokens, queries, kv_weight, out_grad):
    head_width = HEADS * HD
    sequences = TOKENS // LENGTH
    blocks = LENGTH // TOK_DEV
    positions = jnp.arange(TOK_DEV)
    causal = (positions[:, None] >= positions[None, :]).astype(jnp.float32)[None]

    def one_sequence(summed, inputs):
        seq_tokens, seq_queries, seq_grad = inputs
        kv_local = jnp.dot(seq_tokens, kv_weight, preferred_element_type=jnp.float32).astype(jnp.bfloat16)
        query_f = seq_queries.astype(jnp.float32)
        key_f = kv_local[:, :head_width].astype(jnp.float32)
        value_f = kv_local[:, head_width:].astype(jnp.float32).reshape(blocks, TOK_DEV, HEADS, HD)
        q_feat = feature(query_f).reshape(blocks, TOK_DEV, HEADS, HD)
        k_feat = feature(key_f).reshape(blocks, TOK_DEV, HEADS, HD)

        def forward(carried, block_in):
            q_block, k_block, v_block = block_in
            scores = contract('thd,shd->hts', q_block, k_block) * causal
            attended = contract('hts,she->the', scores, v_block) + contract('thd,hde->the', q_block, carried)
            return (carried + contract('thd,the->hde', k_block, v_block), (attended, carried))
        zero_state = jnp.zeros((HEADS, HD, HD), jnp.float32)
        _, (attended, before) = lax.scan(forward, zero_state, (q_feat, k_feat, value_f))
        radius = jnp.sqrt(lax.optimization_barrier(jnp.mean(attended * attended, axis=-1, keepdims=True)) + epsilon)
        normed = attended / radius
        output = normed.astype(jnp.bfloat16).reshape(LENGTH, head_width)
        grad_f = seq_grad.astype(jnp.float32).reshape(blocks, TOK_DEV, HEADS, HD)
        grad_att = (grad_f - normed * lax.optimization_barrier(jnp.mean(grad_f * normed, axis=-1, keepdims=True))) / radius

        def backward(carried, block_in):
            q_block, k_block, v_block, g_block, prior = block_in
            scores = contract('thd,shd->hts', q_block, k_block) * causal
            mixed_w = contract('the,she->hts', g_block, v_block) * causal
            grad_qf = contract('hts,shd->thd', mixed_w, k_block) + contract('the,hde->thd', g_block, prior)
            grad_kf = contract('hts,thd->shd', mixed_w, q_block) + contract('she,hde->shd', v_block, carried)
            grad_val = contract('hts,the->she', scores, g_block) + contract('shd,hde->she', k_block, carried)
            return (carried + contract('thd,the->hde', q_block, g_block), (grad_qf, grad_kf, grad_val))
        _, (grad_qf, grad_kf, grad_val) = lax.scan(backward, zero_state, (q_feat, k_feat, value_f, grad_att, before), reverse=True)
        query_grad = (grad_qf.reshape(LENGTH, head_width) * feature_slope(query_f)).astype(jnp.bfloat16)
        key_grad = (grad_kf.reshape(LENGTH, head_width) * feature_slope(key_f)).astype(jnp.bfloat16)
        kv_grad = jnp.concatenate([key_grad, grad_val.reshape(LENGTH, head_width).astype(jnp.bfloat16)], axis=1)
        token_grad = lax.dot_general(kv_grad, kv_weight, (((1,), (1,)), ((), ())), preferred_element_type=jnp.float32).astype(jnp.bfloat16)
        summed = summed + lax.dot_general(seq_tokens, kv_grad, (((0,), (0,)), ((), ())), preferred_element_type=jnp.float32)
        return (summed, (output, token_grad, query_grad))
    grads, (outputs, token_grads, query_grads) = lax.scan(one_sequence, jnp.zeros((D, 2 * head_width), jnp.float32), (tokens.reshape(sequences, LENGTH, D), queries.reshape(sequences, LENGTH, head_width), out_grad.reshape(sequences, LENGTH, head_width)))
    weight_grad = grads * (1.0 / jnp.sqrt(jnp.float32(TOKENS)))
    return (outputs.reshape(TOKENS, head_width), token_grads.reshape(TOKENS, D), query_grads.reshape(TOKENS, head_width), weight_grad)
```

```python
import math

import jax
import jax.numpy as jnp
from jax import lax
from jax.sharding import PartitionSpec as P

HEADS = 8
HD = 128


epsilon = 1e-05


def prefix(x, axis, combine, identity, reverse):
    size, place = (lax.axis_size(axis), lax.axis_index(axis))
    everything = lax.all_gather(x.astype(jnp.bfloat16), axis)
    start = jnp.broadcast_to(jnp.asarray(identity, x.dtype), x.shape)

    def lap(k, before):
        at = size - 1 - k if reverse else k
        reached = at > place if reverse else at < place
        new = combine(before, everything[at].astype(x.dtype))
        return jnp.where(reached, new, before)

    return lax.fori_loop(0, size, lap, start)


def feature(inputs):
    return jnp.where(inputs > 0, inputs + 1.0, jnp.exp(jnp.minimum(inputs, 0.0)))


def feature_slope(inputs):
    return jnp.where(inputs > 0, 1.0, jnp.exp(jnp.minimum(inputs, 0.0)))


def contract(formula, first_op, second_op):
    return jnp.einsum(
        formula,
        first_op.astype(jnp.bfloat16),
        second_op.astype(jnp.bfloat16),
        preferred_element_type=jnp.float32,
    )


def add_states(earlier, latter):
    return earlier + latter


def on_device(tokens, queries, kv_weight, out_grad):
    local_rows = tokens.shape[0]
    head_width = HEADS * HD
    weights = lax.all_gather(kv_weight, "seq", axis=0, tiled=True)
    kv_local = jnp.dot(tokens, weights, preferred_element_type=jnp.float32).astype(jnp.bfloat16)
    query_f = queries.astype(jnp.float32)
    key_f = kv_local[:, :head_width].astype(jnp.float32)
    value_f = kv_local[:, head_width:].astype(jnp.float32).reshape(local_rows, HEADS, HD)
    q_feat = feature(query_f).reshape(local_rows, HEADS, HD)
    k_feat = feature(key_f).reshape(local_rows, HEADS, HD)
    positions = jnp.arange(local_rows)
    causal = (positions[:, None] >= positions[None, :]).astype(jnp.float32)[None]
    zero_state = jnp.zeros((HEADS, HD, HD), jnp.float32)
    own_state = contract("thd,the->hde", k_feat, value_f)
    before = prefix(own_state, "seq", add_states, zero_state, False)
    scores = contract("thd,shd->hts", q_feat, k_feat) * causal
    attended = contract("hts,she->the", scores, value_f) + contract("thd,hde->the", q_feat, before)
    radius = jnp.sqrt(jnp.mean(attended * attended, axis=-1, keepdims=True) + epsilon)
    normed = attended / radius
    output = normed.astype(jnp.bfloat16).reshape(local_rows, head_width)
    grad_f = out_grad.astype(jnp.float32).reshape(local_rows, HEADS, HD)
    grad_att = (grad_f - normed * jnp.mean(grad_f * normed, axis=-1, keepdims=True)) / radius
    own_grad = contract("thd,the->hde", q_feat, grad_att)
    later_sum = prefix(own_grad, "seq", add_states, zero_state, True)
    mixed_w = contract("the,she->hts", grad_att, value_f) * causal
    grad_qf = contract("hts,shd->thd", mixed_w, k_feat) + contract("the,hde->thd", grad_att, before)
    grad_kf = contract("hts,thd->shd", mixed_w, q_feat) + contract(
        "she,hde->shd", value_f, later_sum
    )
    grad_val = contract("hts,the->she", scores, grad_att) + contract(
        "shd,hde->she", k_feat, later_sum
    )
    query_grad = (grad_qf.reshape(local_rows, head_width) * feature_slope(query_f)).astype(
        jnp.bfloat16
    )
    key_grad = (grad_kf.reshape(local_rows, head_width) * feature_slope(key_f)).astype(jnp.bfloat16)
    kv_grad = jnp.concatenate(
        [key_grad, grad_val.reshape(local_rows, head_width).astype(jnp.bfloat16)], axis=1
    )
    token_grad = lax.dot_general(
        kv_grad, weights, (((1,), (1,)), ((), ())), preferred_element_type=jnp.float32
    ).astype(jnp.bfloat16)
    batch_count = lax.axis_size("dp")
    shard_count = lax.axis_size("seq")
    grad_scale = 1.0 / math.sqrt(local_rows * batch_count * shard_count)
    partial_grad = lax.psum_scatter(
        (
            lax.dot_general(
                tokens, kv_grad, (((0,), (0,)), ((), ())), preferred_element_type=jnp.float32
            )
            * grad_scale
        ).astype(jnp.bfloat16),
        "dp",
        scatter_dimension=0,
        tiled=True,
    )
    weight_grad = lax.psum_scatter(partial_grad, "seq", scatter_dimension=0, tiled=True).astype(
        jnp.float32
    )
    return (output, token_grad, query_grad, weight_grad)


def solution(mesh):
    in_specs = (
        P(("dp", "seq"), None),
        P(("dp", "seq"), None),
        P("seq", None),
        P(("dp", "seq"), None),
    )
    out_specs = (
        P(("dp", "seq"), None),
        P(("dp", "seq"), None),
        P(("dp", "seq"), None),
        P(("dp", "seq"), None),
    )
    return jax.shard_map(
        on_device, mesh=mesh, in_specs=in_specs, out_specs=out_specs, check_vma=False
    )
```

```python
import functools
import math

import jax
import jax.numpy as jnp
from jax import lax
from jax.experimental import pallas as pl
from jax.experimental.pallas import tpu as pltpu
from jax.sharding import PartitionSpec as P

HEADS = 8
HD = 128
EPS = 1e-05
MESH = pl.DeviceIdType.MESH
BF = jnp.bfloat16
F32 = jnp.float32


def dot(a, b, ca, cb):
    return lax.dot_general(a, b, (((ca,), (cb,)), ((), ())), preferred_element_type=F32)


def feature(u):
    return jnp.where(u > 0, u + 1.0, jnp.exp(jnp.minimum(u, 0.0)))


def slope(u):
    return jnp.where(u > 0, 1.0, jnp.exp(jnp.minimum(u, 0.0)))


def bit_of(x, b):
    return (x // (1 << b)) % 2


def flip(x, mask):
    b = 0
    while mask >> b:
        if (mask >> b) & 1:
            x = x + (1 << b) * (1 - 2 * bit_of(x, b))
        b += 1
    return x


def span(bits):
    masks = [0]
    for b in bits:
        masks = masks + [m | (1 << b) for m in masks]
    return masks


def kernel(
    N, Z, S, scale,
    tok, q_ref, w_ref, og_ref,
    o_ref, tg_ref, qg_ref, wg_ref,
    wfull, kvacc, kv, kvg, tokt, ga_buf, sc_buf, mw_buf, bef_buf, fsnd, lat_buf, bsnd, owng,
    part, *rest,
):
    nb = N.bit_length() - 1
    gb = S.bit_length() - 1
    rbufs = rest[:nb]
    (fin, zbuf, loc_sem, zs_sem, zr_sem, ps_sem, pr_sem, fs_sem, fr_sem, bs_sem, br_sem,
     rs_sem, rr_sem, es_sem, er_sem) = rest[nb:]
    me = lax.axis_index("dp")
    z = lax.axis_index("seq")
    T = tok.shape[0]
    D = tok.shape[1]
    HW = HEADS * HD
    R = D // Z
    sl = me % S

    def dev(dp, zz):
        return (dp, zz)

    def up(k):
        return lax.rem(z + k, Z)

    def down(k):
        return lax.rem(z + Z - k, Z)

    barrier = pltpu.get_barrier_semaphore()
    for b in range(nb):
        pl.semaphore_signal(barrier, inc=1, device_id=dev(flip(me, 1 << b), z), device_id_type=MESH)
    for k in range(1, Z):
        pl.semaphore_signal(barrier, inc=1, device_id=dev(me, up(k)), device_id_type=MESH)
    pl.semaphore_wait(barrier, nb + Z - 1)

    def zcopy(k, p):
        return pltpu.make_async_remote_copy(
            src_ref=w_ref.at[sl, :, pl.ds(p * HW, HW)], dst_ref=wfull.at[z, p, sl],
            send_sem=zs_sem.at[k, p], recv_sem=zr_sem.at[k, p],
            device_id=dev(me, up(k)), device_id_type=MESH)

    def zland(k, p):
        o = down(k)
        return pltpu.make_async_remote_copy(
            src_ref=w_ref.at[sl, :, pl.ds(p * HW, HW)], dst_ref=wfull.at[o, p, sl],
            send_sem=zs_sem.at[k, p], recv_sem=zr_sem.at[k, p],
            device_id=dev(me, up(k)), device_id_type=MESH)

    gorder = [list(range(1, gb)) + [0], list(range(gb - 1, 0, -1)) + [0]]

    def pcopy(k, p, mask, b, landed=False):
        o = down(k)
        s_src = flip(sl, mask | (1 << b) if landed else mask)
        return pltpu.make_async_remote_copy(
            src_ref=wfull.at[o, p, s_src], dst_ref=wfull.at[o, p, s_src],
            send_sem=ps_sem.at[k, p, mask | (1 << b)], recv_sem=pr_sem.at[k, p, mask | (1 << b)],
            device_id=dev(flip(me, 1 << b), z), device_id_type=MESH)

    def mm(o, first=False):
        t = tok[:, pl.ds(pl.multiple_of(o * R, 128), R)]
        for p in range(2):
            prod = dot(t, wfull[o, p].reshape(R, HW), 1, 0)
            cols = slice(p * HW, (p + 1) * HW)
            if first:
                kvacc[:, cols] = prod
            else:
                kvacc[:, cols] += prod

    for k in range(1, Z):
        for p in range(2):
            zcopy(k, p).start()
    loc = [pltpu.make_async_copy(w_ref.at[:, :, pl.ds(p * HW, HW)], wfull.at[z, p], loc_sem.at[p]) for p in range(2)]
    for c in loc:
        c.start()
    for c0 in range(0, D, 256):
        tokt[c0:c0 + 256, :] = tok[:, c0:c0 + 256].T

    @pl.when(z == 0)
    def _():
        bef_buf[...] = jnp.zeros_like(bef_buf)

    @pl.when(z == Z - 1)
    def _():
        lat_buf[...] = jnp.zeros_like(lat_buf)

    for c in loc:
        c.wait()
    mm(z, True)
    for t in range(Z - 1 + gb):
        for j in range(gb, -1, -1):
            k = t - j + 1
            if not 1 <= k <= Z - 1:
                continue
            for p in range(2):
                bits = gorder[p]
                if j == 0:
                    zland(k, p).wait_recv()
                else:
                    for mask in span(bits[:j - 1]):
                        pcopy(k, p, mask, bits[j - 1], True).wait_recv()
                if j < gb:
                    for mask in span(bits[:j]):
                        pcopy(k, p, mask, bits[j]).start()
            if j == gb:
                mm(down(k))
    kv[...] = kvacc[...].astype(BF)

    row = lax.broadcasted_iota(jnp.int32, (T, T), 0)
    col = lax.broadcasted_iota(jnp.int32, (T, T), 1)
    causal = row >= col

    def cols_of(h):
        return (pl.ds(pl.multiple_of(h * HD, HD), HD), pl.ds(pl.multiple_of(HW + h * HD, HD), HD))

    def fcopy(h):
        return pltpu.make_async_remote_copy(
            src_ref=fsnd.at[h], dst_ref=bef_buf.at[h], send_sem=fs_sem.at[h], recv_sem=fr_sem.at[h],
            device_id=dev(me, up(1)), device_id_type=MESH)

    def bcopy(h):
        return pltpu.make_async_remote_copy(
            src_ref=bsnd.at[h], dst_ref=lat_buf.at[h], send_sem=bs_sem.at[h], recv_sem=br_sem.at[h],
            device_id=dev(me, down(1)), device_id_type=MESH)

    def forward(h, _):
        hs, vs = cols_of(h)
        kf = feature(kv[:, hs].astype(F32)).astype(BF)
        qf = feature(q_ref[:, hs].astype(F32)).astype(BF)
        v = kv[:, vs]
        own = dot(kf, v, 0, 0)

        @pl.when(z > 0)
        def _():
            fcopy(h).wait_recv()

        bef = bef_buf[h]

        @pl.when(z < Z - 1)
        def _():
            fsnd[h] = (bef.astype(F32) + own).astype(BF)
            fcopy(h).start()

        sc = jnp.where(causal, dot(qf, kf, 1, 1), 0.0).astype(BF)
        sc_buf[h] = sc
        att = dot(sc, v, 1, 0) + dot(qf, bef, 1, 0)
        rinv = lax.rsqrt(jnp.mean(att * att, axis=-1, keepdims=True) + EPS)
        normed = att * rinv
        o_ref[:, hs] = normed.astype(BF)
        g = og_ref[:, hs].astype(F32)
        ga = ((g - normed * jnp.mean(g * normed, axis=-1, keepdims=True)) * rinv).astype(BF)
        ga_buf[:, hs] = ga
        og = dot(qf, ga, 0, 0)
        owng[h] = og

        @pl.when(z == Z - 1)
        def _():
            bsnd[h] = og.astype(BF)
            bcopy(h).start()

        return 0

    lax.fori_loop(0, HEADS, forward, 0)

    order = [list(range(nb)), [0] + list(range(nb - 1, 0, -1))]

    def slot_of(mask, bits):
        s = 0
        for j, b in enumerate(bits):
            if (mask >> b) & 1:
                s += N >> (j + 1)
        return s

    def rcopy(h, p, j):
        half = N >> (j + 1)
        return pltpu.make_async_remote_copy(
            src_ref=part.at[h, p, pl.ds(half, half)], dst_ref=rbufs[j].at[h, p],
            send_sem=rs_sem.at[h, p, j], recv_sem=rr_sem.at[h, p, j],
            device_id=dev(flip(me, 1 << order[p][j]), z), device_id_type=MESH)

    def ecopy(h, k):
        return pltpu.make_async_remote_copy(
            src_ref=fin.at[h, up(k)], dst_ref=zbuf.at[h, k],
            send_sem=es_sem.at[h, k], recv_sem=er_sem.at[h, k],
            device_id=dev(me, up(k)), device_id_type=MESH)

    rd = D // N
    rb = rd // Z

    def backward(h):
        hs, vs = cols_of(h)

        @pl.when(z < Z - 1)
        def _():
            bcopy(h).wait_recv()

        lat = lat_buf[h]

        @pl.when(jnp.logical_and(z > 0, z < Z - 1))
        def _():
            bsnd[h] = (lat.astype(F32) + owng[h]).astype(BF)
            bcopy(h).start()

        key = kv[:, hs].astype(F32)
        kf = feature(key).astype(BF)
        qf = feature(q_ref[:, hs].astype(F32)).astype(BF)
        v = kv[:, vs]
        ga = ga_buf[:, hs]
        mw = jnp.where(causal, dot(ga, v, 1, 1), 0.0).astype(BF)
        mw_buf[h] = mw
        gk = dot(mw, qf, 0, 0) + dot(v, lat, 1, 1)
        gv = dot(sc_buf[h], ga, 0, 0) + dot(kf, lat, 1, 0)
        gkb = (gk * slope(key)).astype(BF)
        gvb = gv.astype(BF)
        kvg[:, hs] = gkb
        kvg[:, vs] = gvb
        chunk = jnp.concatenate([gkb, gvb], axis=1)
        for m in range(N):
            d = flip(me, m)
            res = dot(tokt[pl.ds(pl.multiple_of(d * rd, rd), rd), :], chunk, 1, 0) * scale
            res = res.reshape(Z, rb, 2 * HD).astype(BF)
            for p in range(2):
                part[h, p, slot_of(m, order[p])] = res[:, :, p * HD:(p + 1) * HD]
        for p in range(2):
            rcopy(h, p, 0).start()

    def stage(h, j):
        for p in range(2):
            half = N >> j
            rcopy(h, p, j - 1).wait_recv()
            if j < nb:
                part[h, p, 0:half] = part[h, p, 0:half] + rbufs[j - 1][h, p]
                rcopy(h, p, j).start()
            else:
                fin[h, :, p] = part[h, p, 0] + rbufs[j - 1][h, p, 0]
        if j == nb:
            for k in range(1, Z):
                ecopy(h, k).start()

    def finish(h):
        hs, vs = cols_of(h)
        total = fin[h, z].astype(F32)
        for k in range(1, Z):
            ecopy(h, k).wait_recv()
            total = total + zbuf[h, k].astype(F32)
        wg_ref[:, hs] = total[0]
        wg_ref[:, vs] = total[1]
        for k in range(1, Z):
            ecopy(h, k).wait_send()
        for p in range(2):
            for j in range(nb):
                rcopy(h, p, j).wait_send()

    def token_part(zz, _):
        w = wfull[zz]
        a = dot(kvg[:, :HW], w[0].reshape(R, HW), 1, 1)
        a = a + dot(kvg[:, HW:], w[1].reshape(R, HW), 1, 1)
        tg_ref[:, pl.ds(pl.multiple_of(zz * R, 128), R)] = a.astype(BF)
        return 0

    def query_part(h, _):
        hs, vs = cols_of(h)
        kf = feature(kv[:, hs].astype(F32)).astype(BF)
        gq = dot(mw_buf[h], kf, 1, 0) + dot(ga_buf[:, hs], bef_buf[h], 1, 1)
        qg_ref[:, hs] = (gq * slope(q_ref[:, hs].astype(F32))).astype(BF)
        return 0

    def lap(it, _):
        @pl.when(it < HEADS)
        def _():
            backward(it)

        for j in range(1, nb + 1):
            @pl.when(jnp.logical_and(it >= j, it < HEADS + j))
            def _(j=j):
                stage(it - j, j)

        @pl.when(it >= nb + 1)
        def _():
            finish(it - nb - 1)

        @pl.when(it == HEADS)
        def _():
            lax.fori_loop(0, Z, token_part, 0)

        @pl.when(it == HEADS + 1)
        def _():
            lax.fori_loop(0, HEADS, query_part, 0)

        return 0

    lax.fori_loop(0, HEADS + nb + 1, lap, 0)

    for k in range(1, Z):
        for p in range(2):
            zcopy(k, p).wait_send()
            bits = gorder[p]
            for j, b in enumerate(bits):
                for mask in span(bits[:j]):
                    pcopy(k, p, mask, b).wait_send()

    @pl.when(z < Z - 1)
    def _():
        def w(h, _):
            fcopy(h).wait_send()
            return 0
        lax.fori_loop(0, HEADS, w, 0)

    @pl.when(z > 0)
    def _():
        def w(h, _):
            bcopy(h).wait_send()
            return 0
        lax.fori_loop(0, HEADS, w, 0)


def solution(mesh):
    N = mesh.shape["dp"]
    Z = mesh.shape["seq"]

    def on_device(tokens, queries, kv_weight, out_grad):
        T, D = tokens.shape
        R = kv_weight.shape[0]
        HW = queries.shape[1]
        S = min(N, R // 16)
        r = R // S
        nb = N.bit_length() - 1
        rd = D // N
        rb = rd // Z
        scale = 1.0 / math.sqrt(T * N * Z)
        vm = pl.BlockSpec(memory_space=pltpu.VMEM)
        dma = pltpu.SemaphoreType.DMA
        scratch = [
            pltpu.VMEM((Z, 2, S, r, HW), BF),
            pltpu.VMEM((T, 2 * HW), F32),
            pltpu.VMEM((T, 2 * HW), BF),
            pltpu.VMEM((T, 2 * HW), BF),
            pltpu.VMEM((D, T), BF),
            pltpu.VMEM((T, HW), BF),
            pltpu.VMEM((HEADS, T, T), BF),
            pltpu.VMEM((HEADS, T, T), BF),
            pltpu.VMEM((HEADS, HD, HD), BF),
            pltpu.VMEM((HEADS, HD, HD), BF),
            pltpu.VMEM((HEADS, HD, HD), BF),
            pltpu.VMEM((HEADS, HD, HD), BF),
            pltpu.VMEM((HEADS, HD, HD), F32),
            pltpu.VMEM((HEADS, 2, N, Z, rb, HD), BF),
        ]
        scratch += [pltpu.VMEM((HEADS, 2, N >> (j + 1), Z, rb, HD), BF) for j in range(nb)]
        scratch += [
            pltpu.VMEM((HEADS, Z, 2, rb, HD), BF),
            pltpu.VMEM((HEADS, Z, 2, rb, HD), BF),
            dma((2,)),
            dma((Z, 2)), dma((Z, 2)),
            dma((Z, 2, S)), dma((Z, 2, S)),
            dma((HEADS,)), dma((HEADS,)),
            dma((HEADS,)), dma((HEADS,)),
            dma((HEADS, 2, nb)), dma((HEADS, 2, nb)),
            dma((HEADS, Z)), dma((HEADS, Z)),
        ]
        return pl.pallas_call(
            functools.partial(kernel, N, Z, S, scale),
            out_shape=(
                jax.ShapeDtypeStruct((T, HW), BF),
                jax.ShapeDtypeStruct((T, D), BF),
                jax.ShapeDtypeStruct((T, HW), BF),
                jax.ShapeDtypeStruct((rb, 2 * HW), F32),
            ),
            in_specs=[vm] * 4,
            out_specs=(vm,) * 4,
            scratch_shapes=scratch,
            compiler_params=pltpu.CompilerParams(
                collective_id=0, has_side_effects=True, vmem_limit_bytes=58 * 1024 * 1024
            ),
            cost_estimate=pl.CostEstimate(flops=8 * T * D * HW * 2, bytes_accessed=8 * T * D, transcendentals=T * HW * 4),
        )(tokens, queries, kv_weight.reshape(S, r, 2 * HW), out_grad)

    spec = P(("dp", "seq"), None)
    return jax.shard_map(
        on_device, mesh=mesh, in_specs=(spec, spec, P("seq", None), spec),
        out_specs=(spec,) * 4, check_vma=False,
    )
```

```python
import functools
import math

import jax
import jax.numpy as jnp
from jax import lax
from jax.experimental import pallas as pl
from jax.experimental.pallas import tpu as pltpu
from jax.sharding import PartitionSpec as P

HEADS = 8
HD = 128
CHUNK = 2
EPS = 1e-05
MESH = pl.DeviceIdType.MESH
BF = jnp.bfloat16
F32 = jnp.float32


def dot(a, b, ca, cb):
    return lax.dot_general(a, b, (((ca,), (cb,)), ((), ())), preferred_element_type=F32)


def feature(u):
    return jnp.where(u > 0, u + 1.0, jnp.exp(jnp.minimum(u, 0.0)))


def slope(u):
    return jnp.where(u > 0, 1.0, jnp.exp(jnp.minimum(u, 0.0)))


def bit_of(x, b):
    return (x // (1 << b)) % 2


def flip(x, mask):
    b = 0
    while mask >> b:
        if (mask >> b) & 1:
            x = x + (1 << b) * (1 - 2 * bit_of(x, b))
        b += 1
    return x


def kernel(
    N, Z, S, scale,
    tok, q_ref, w_ref, og_ref,
    o_ref, tg_ref, qg_ref, wg_ref,
    wfull, kv, kvg, tokt, ga_buf, sc_buf, mw_buf, bef_buf, fsnd, lat_buf, bsnd, owng,
    part, *rest,
):
    nb = N.bit_length() - 1
    gb = S.bit_length() - 1
    rbufs = rest[:nb]
    (fin, zbuf, loc_sem, zs_sem, zr_sem, ps_sem, pr_sem, fs_sem, fr_sem, bs_sem, br_sem,
     rs_sem, rr_sem, es_sem, er_sem) = rest[nb:]
    me = lax.axis_index("dp")
    z = lax.axis_index("seq")
    T = tok.shape[0]
    D = tok.shape[1]
    HW = HEADS * HD
    R = D // Z
    sl = me % S

    def dev(dp, zz):
        return (dp, zz)

    def up(k):
        return lax.rem(z + k, Z)

    def down(k):
        return lax.rem(z + Z - k, Z)

    barrier = pltpu.get_barrier_semaphore()
    for b in range(nb):
        pl.semaphore_signal(barrier, inc=1, device_id=dev(flip(me, 1 << b), z), device_id_type=MESH)
    for k in range(1, Z):
        pl.semaphore_signal(barrier, inc=1, device_id=dev(me, up(k)), device_id_type=MESH)
    pl.semaphore_wait(barrier, nb + Z - 1)

    CW = CHUNK * HD
    C = HEADS // CHUNK

    def place(spread, flipped=None):
        at = []
        for b in reversed(range(gb)):
            if b in spread:
                at.append(slice(None))
            else:
                at.append(1 - bit_of(sl, b) if b == flipped else bit_of(sl, b))
        return tuple(at)

    def chunk_cols(c, p):
        return pl.ds(pl.multiple_of(p * HW + c * CW, CW), CW)

    def zcopy(c, k, p, landed=False):
        return pltpu.make_async_remote_copy(
            src_ref=w_ref.at[place(()) + (slice(None), chunk_cols(c, p))],
            dst_ref=wfull.at[(c, p, down(k) if landed else z) + place(())],
            send_sem=zs_sem.at[c, k, p], recv_sem=zr_sem.at[c, k, p],
            device_id=dev(me, up(k)), device_id_type=MESH)

    gorder = [list(range(1, gb)) + [0], list(range(gb - 1, 0, -1)) + [0]]

    def pcopy(c, k, p, j, landed=False):
        bits = gorder[p]
        src = wfull.at[(c, p, down(k)) + place(bits[:j])]
        dst = wfull.at[(c, p, down(k)) + place(bits[:j], bits[j])] if landed else src
        return pltpu.make_async_remote_copy(
            src_ref=src, dst_ref=dst,
            send_sem=ps_sem.at[c, k, p, j], recv_sem=pr_sem.at[c, k, p, j],
            device_id=dev(flip(me, 1 << bits[j]), z), device_id_type=MESH)

    def send_chunk(c):
        for k in range(1, Z):
            for p in range(2):
                zcopy(c, k, p).start()

    def loc(c, p):
        return pltpu.make_async_copy(
            w_ref.at[(slice(None),) * (gb + 1) + (chunk_cols(c, p),)], wfull.at[c, p, z], loc_sem.at[c, p])

    for c in range(2):
        send_chunk(c)
    for c in range(C):
        for p in range(2):
            loc(c, p).start()
    for c0 in range(0, D, 256):
        tokt[c0:c0 + 256, :] = tok[:, c0:c0 + 256].T

    @pl.when(z == 0)
    def _():
        bef_buf[...] = jnp.zeros_like(bef_buf)

    @pl.when(z == Z - 1)
    def _():
        lat_buf[...] = jnp.zeros_like(lat_buf)

    for c in range(C):
        for p in range(2):
            loc(c, p).wait()

    def serve(c, k, j):
        for p in range(2):
            if j == 0:
                zcopy(c, k, p, True).wait_recv()
            else:
                pcopy(c, k, p, j - 1, True).wait_recv()
            if j < gb:
                pcopy(c, k, p, j).start()

    def project(c):
        for p in range(2):
            prod = dot(tok[...], wfull[c, p].reshape(D, CW), 1, 0)
            kv[:, chunk_cols(c, p)] = prod.astype(BF)

    row = lax.broadcasted_iota(jnp.int32, (T, T), 0)
    col = lax.broadcasted_iota(jnp.int32, (T, T), 1)
    causal = row >= col

    def cols_of(h):
        return (pl.ds(pl.multiple_of(h * HD, HD), HD), pl.ds(pl.multiple_of(HW + h * HD, HD), HD))

    def fcopy(h):
        return pltpu.make_async_remote_copy(
            src_ref=fsnd.at[h], dst_ref=bef_buf.at[h], send_sem=fs_sem.at[h], recv_sem=fr_sem.at[h],
            device_id=dev(me, up(1)), device_id_type=MESH)

    def bcopy(h):
        return pltpu.make_async_remote_copy(
            src_ref=bsnd.at[h], dst_ref=lat_buf.at[h], send_sem=bs_sem.at[h], recv_sem=br_sem.at[h],
            device_id=dev(me, down(1)), device_id_type=MESH)

    def forward(h, _):
        hs, vs = cols_of(h)
        kf = feature(kv[:, hs].astype(F32)).astype(BF)
        qf = feature(q_ref[:, hs].astype(F32)).astype(BF)
        v = kv[:, vs]
        own = dot(kf, v, 0, 0)

        @pl.when(z > 0)
        def _():
            fcopy(h).wait_recv()

        bef = bef_buf[h]

        @pl.when(z < Z - 1)
        def _():
            fsnd[h] = (bef.astype(F32) + own).astype(BF)
            fcopy(h).start()

        sc = jnp.where(causal, dot(qf, kf, 1, 1), 0.0).astype(BF)
        sc_buf[h] = sc
        att = dot(sc, v, 1, 0) + dot(qf, bef, 1, 0)
        rinv = lax.rsqrt(jnp.mean(att * att, axis=-1, keepdims=True) + EPS)
        normed = att * rinv
        o_ref[:, hs] = normed.astype(BF)
        g = og_ref[:, hs].astype(F32)
        ga = ((g - normed * jnp.mean(g * normed, axis=-1, keepdims=True)) * rinv).astype(BF)
        ga_buf[:, hs] = ga
        og = dot(qf, ga, 0, 0)
        owng[h] = og

        @pl.when(z == Z - 1)
        def _():
            bsnd[h] = og.astype(BF)
            bcopy(h).start()

    def pass_back(h):
        @pl.when(z < Z - 1)
        def _():
            bcopy(h).wait_recv()

        @pl.when(jnp.logical_and(z > 0, z < Z - 1))
        def _():
            bsnd[h] = (lat_buf[h].astype(F32) + owng[h]).astype(BF)
            bcopy(h).start()

    def gather_lap(it, _):
        for k in range(1, Z):
            if k == 1:
                @pl.when(it + 2 < C)
                def _():
                    send_chunk(it + 2)
            for j in range(gb, -1, -1):
                dc = (k - 1 - j) // (Z - 1)
                kk = (k - 1 - j) % (Z - 1) + 1
                c = it + dc

                @pl.when(jnp.logical_and(c >= 0, c < C))
                def _(c=c, kk=kk, j=j):
                    serve(c, kk, j)
                    if j == gb and kk == Z - 1:
                        project(c)
                        forward(c * CHUNK, 0)

            if k == 1:
                @pl.when(it >= 2)
                def _():
                    def more(i, _):
                        forward((it - 2) * CHUNK + i, 0)
                        return 0
                    lax.fori_loop(1, CHUNK, more, 0)

        @pl.when(it >= 3)
        def _():
            for i in range(CHUNK):
                pass_back((it - 3) * CHUNK + i)

        return 0

    lax.fori_loop(0, C + 2, gather_lap, 0)

    order = [list(range(nb)), [0] + list(range(nb - 1, 0, -1))]

    def slot_of(mask, bits):
        s = 0
        for j, b in enumerate(bits):
            if (mask >> b) & 1:
                s += N >> (j + 1)
        return s

    def rcopy(h, p, j):
        half = N >> (j + 1)
        return pltpu.make_async_remote_copy(
            src_ref=part.at[h, p, pl.ds(half, half)], dst_ref=rbufs[j].at[h, p],
            send_sem=rs_sem.at[h, p, j], recv_sem=rr_sem.at[h, p, j],
            device_id=dev(flip(me, 1 << order[p][j]), z), device_id_type=MESH)

    def ecopy(h, k):
        return pltpu.make_async_remote_copy(
            src_ref=fin.at[h, up(k)], dst_ref=zbuf.at[h, k],
            send_sem=es_sem.at[h, k], recv_sem=er_sem.at[h, k],
            device_id=dev(me, up(k)), device_id_type=MESH)

    rd = D // N
    rb = rd // Z

    def backward(h):
        hs, vs = cols_of(h)

        lat = lat_buf[h]
        key = kv[:, hs].astype(F32)
        kf = feature(key).astype(BF)
        qf = feature(q_ref[:, hs].astype(F32)).astype(BF)
        v = kv[:, vs]
        ga = ga_buf[:, hs]
        mw = jnp.where(causal, dot(ga, v, 1, 1), 0.0).astype(BF)
        mw_buf[h] = mw
        gk = dot(mw, qf, 0, 0) + dot(v, lat, 1, 1)
        gv = dot(sc_buf[h], ga, 0, 0) + dot(kf, lat, 1, 0)
        gkb = (gk * slope(key)).astype(BF)
        gvb = gv.astype(BF)
        kvg[:, hs] = gkb
        kvg[:, vs] = gvb
        chunk = jnp.concatenate([gkb, gvb], axis=1)
        for m in range(N):
            d = flip(me, m)
            res = dot(tokt[pl.ds(pl.multiple_of(d * rd, rd), rd), :], chunk, 1, 0) * scale
            res = res.reshape(Z, rb, 2 * HD).astype(BF)
            for p in range(2):
                part[h, p, slot_of(m, order[p])] = res[:, :, p * HD:(p + 1) * HD]
        for p in range(2):
            rcopy(h, p, 0).start()

    def stage(h, j):
        for p in range(2):
            half = N >> j
            rcopy(h, p, j - 1).wait_recv()
            if j < nb:
                part[h, p, 0:half] = part[h, p, 0:half] + rbufs[j - 1][h, p]
                rcopy(h, p, j).start()
            else:
                fin[h, :, p] = part[h, p, 0] + rbufs[j - 1][h, p, 0]
        if j == nb:
            for k in range(1, Z):
                ecopy(h, k).start()

    def finish(h):
        hs, vs = cols_of(h)
        total = fin[h, z].astype(F32)
        for k in range(1, Z):
            ecopy(h, k).wait_recv()
            total = total + zbuf[h, k].astype(F32)
        wg_ref[:, hs] = total[0]
        wg_ref[:, vs] = total[1]
        for k in range(1, Z):
            ecopy(h, k).wait_send()
        for p in range(2):
            for j in range(nb):
                rcopy(h, p, j).wait_send()

    def token_part(zz, _):
        a = jnp.zeros((T, R), F32)
        for c in range(C):
            for p in range(2):
                cols = slice(p * HW + c * CW, p * HW + (c + 1) * CW)
                a = a + dot(kvg[:, cols], wfull[c, p, zz].reshape(R, CW), 1, 1)
        tg_ref[:, pl.ds(pl.multiple_of(zz * R, 128), R)] = a.astype(BF)
        return 0

    def query_part(h, _):
        hs, vs = cols_of(h)
        kf = feature(kv[:, hs].astype(F32)).astype(BF)
        gq = dot(mw_buf[h], kf, 1, 0) + dot(ga_buf[:, hs], bef_buf[h], 1, 1)
        qg_ref[:, hs] = (gq * slope(q_ref[:, hs].astype(F32))).astype(BF)
        return 0

    def lap(it, _):
        @pl.when(it < CHUNK)
        def _():
            pass_back((C - 1) * CHUNK + it)

        @pl.when(it < HEADS)
        def _():
            backward(it)

        for j in range(1, nb + 1):
            @pl.when(jnp.logical_and(it >= j, it < HEADS + j))
            def _(j=j):
                stage(it - j, j)

        @pl.when(it >= nb + 1)
        def _():
            finish(it - nb - 1)

        @pl.when(it == HEADS)
        def _():
            lax.fori_loop(0, Z, token_part, 0)

        @pl.when(it == HEADS + 1)
        def _():
            lax.fori_loop(0, HEADS, query_part, 0)

        return 0

    lax.fori_loop(0, HEADS + nb + 1, lap, 0)

    def sent(c, _):
        for k in range(1, Z):
            for p in range(2):
                zcopy(c, k, p).wait_send()
                for j in range(gb):
                    pcopy(c, k, p, j).wait_send()
        return 0

    lax.fori_loop(0, C, sent, 0)

    @pl.when(z < Z - 1)
    def _():
        def w(h, _):
            fcopy(h).wait_send()
            return 0
        lax.fori_loop(0, HEADS, w, 0)

    @pl.when(z > 0)
    def _():
        def w(h, _):
            bcopy(h).wait_send()
            return 0
        lax.fori_loop(0, HEADS, w, 0)


def solution(mesh):
    N = mesh.shape["dp"]
    Z = mesh.shape["seq"]

    def on_device(tokens, queries, kv_weight, out_grad):
        T, D = tokens.shape
        R = kv_weight.shape[0]
        HW = queries.shape[1]
        S = min(N, R // 16)
        r = R // S
        nb = N.bit_length() - 1
        gb = S.bit_length() - 1
        rd = D // N
        rb = rd // Z
        scale = 1.0 / math.sqrt(T * N * Z)
        vm = pl.BlockSpec(memory_space=pltpu.VMEM)
        dma = pltpu.SemaphoreType.DMA
        scratch = [
            pltpu.VMEM((HEADS // CHUNK, 2, Z) + (2,) * gb + (r, CHUNK * HD), BF),
            pltpu.VMEM((T, 2 * HW), BF),
            pltpu.VMEM((T, 2 * HW), BF),
            pltpu.VMEM((D, T), BF),
            pltpu.VMEM((T, HW), BF),
            pltpu.VMEM((HEADS, T, T), BF),
            pltpu.VMEM((HEADS, T, T), BF),
            pltpu.VMEM((HEADS, HD, HD), BF),
            pltpu.VMEM((HEADS, HD, HD), BF),
            pltpu.VMEM((HEADS, HD, HD), BF),
            pltpu.VMEM((HEADS, HD, HD), BF),
            pltpu.VMEM((HEADS, HD, HD), F32),
            pltpu.VMEM((HEADS, 2, N, Z, rb, HD), BF),
        ]
        scratch += [pltpu.VMEM((HEADS, 2, N >> (j + 1), Z, rb, HD), BF) for j in range(nb)]
        scratch += [
            pltpu.VMEM((HEADS, Z, 2, rb, HD), BF),
            pltpu.VMEM((HEADS, Z, 2, rb, HD), BF),
            dma((HEADS // CHUNK, 2)),
            dma((HEADS // CHUNK, Z, 2)), dma((HEADS // CHUNK, Z, 2)),
            dma((HEADS // CHUNK, Z, 2, gb)), dma((HEADS // CHUNK, Z, 2, gb)),
            dma((HEADS,)), dma((HEADS,)),
            dma((HEADS,)), dma((HEADS,)),
            dma((HEADS, 2, nb)), dma((HEADS, 2, nb)),
            dma((HEADS, Z)), dma((HEADS, Z)),
        ]
        return pl.pallas_call(
            functools.partial(kernel, N, Z, S, scale),
            out_shape=(
                jax.ShapeDtypeStruct((T, HW), BF),
                jax.ShapeDtypeStruct((T, D), BF),
                jax.ShapeDtypeStruct((T, HW), BF),
                jax.ShapeDtypeStruct((rb, 2 * HW), F32),
            ),
            in_specs=[vm] * 4,
            out_specs=(vm,) * 4,
            scratch_shapes=scratch,
            compiler_params=pltpu.CompilerParams(
                collective_id=0, has_side_effects=True, vmem_limit_bytes=58 * 1024 * 1024
            ),
            cost_estimate=pl.CostEstimate(flops=8 * T * D * HW * 2, bytes_accessed=8 * T * D, transcendentals=T * HW * 4),
        )(tokens, queries, kv_weight.reshape((2,) * gb + (r, 2 * HW)), out_grad)

    spec = P(("dp", "seq"), None)
    return jax.shard_map(
        on_device, mesh=mesh, in_specs=(spec, spec, P("seq", None), spec),
        out_specs=(spec,) * 4, check_vma=False,
    )
```

```python
import functools
import math

import jax
import jax.numpy as jnp
from jax import lax
from jax.experimental import pallas as pl
from jax.experimental.pallas import tpu as pltpu
from jax.sharding import PartitionSpec as P

HEADS = 8
HD = 128
CHUNK = 4
EPS = 1e-05
MESH = pl.DeviceIdType.MESH
BF = jnp.bfloat16
F32 = jnp.float32


def dot(a, b, ca, cb):
    return lax.dot_general(a, b, (((ca,), (cb,)), ((), ())), preferred_element_type=F32)


def feature(u):
    return jnp.where(u > 0, u + 1.0, jnp.exp(jnp.minimum(u, 0.0)))


def slope(u):
    return jnp.where(u > 0, 1.0, jnp.exp(jnp.minimum(u, 0.0)))


def bit_of(x, b):
    return (x // (1 << b)) % 2


def flip(x, mask):
    b = 0
    while mask >> b:
        if (mask >> b) & 1:
            x = x + (1 << b) * (1 - 2 * bit_of(x, b))
        b += 1
    return x


def kernel(
    N, Z, S, scale,
    tok, q_ref, w_ref, og_ref,
    o_ref, tg_ref, qg_ref, wg_ref,
    wfull, kv, kvg, tokt, ga_buf, sc_buf, mw_buf, bef_buf, fsnd, lat_buf, bsnd, owng,
    part, *rest,
):
    nb = N.bit_length() - 1
    gb = S.bit_length() - 1
    rbufs = rest[:nb]
    (fin, zbuf, loc_sem, zs_sem, zr_sem, ps_sem, pr_sem, fs_sem, fr_sem, bs_sem, br_sem,
     rs_sem, rr_sem, es_sem, er_sem) = rest[nb:]
    me = lax.axis_index("dp")
    z = lax.axis_index("seq")
    T = tok.shape[0]
    D = tok.shape[1]
    HW = HEADS * HD
    R = D // Z
    sl = me % S

    def dev(dp, zz):
        return (dp, zz)

    def up(k):
        return lax.rem(z + k, Z)

    def down(k):
        return lax.rem(z + Z - k, Z)

    barrier = pltpu.get_barrier_semaphore()
    for b in range(nb):
        pl.semaphore_signal(barrier, inc=1, device_id=dev(flip(me, 1 << b), z), device_id_type=MESH)
    for k in range(1, Z):
        pl.semaphore_signal(barrier, inc=1, device_id=dev(me, up(k)), device_id_type=MESH)
    pl.semaphore_wait(barrier, nb + Z - 1)

    CW = CHUNK * HD
    C = HEADS // CHUNK

    def place(spread, flipped=None):
        at = []
        for b in reversed(range(gb)):
            if b in spread:
                at.append(slice(None))
            else:
                at.append(1 - bit_of(sl, b) if b == flipped else bit_of(sl, b))
        return tuple(at)

    def chunk_cols(c, p):
        return pl.ds(pl.multiple_of(p * HW + c * CW, CW), CW)

    def origin(u):
        pairs = jnp.minimum(z, Z - 1 - z)
        near = z - (u + 1) // 2 if u % 2 else z + u // 2
        far = jnp.where(z > Z - 1 - z, z - (u - pairs), z + (u - pairs))
        return jnp.where(u <= 2 * pairs, near, far)

    def zcopy(c, o, p, way, own=False):
        home = wfull.at[(c, p, o) + place(())]
        src = w_ref.at[place(()) + (slice(None), chunk_cols(c, p))] if own else home
        return pltpu.make_async_remote_copy(
            src_ref=src, dst_ref=home,
            send_sem=zs_sem.at[c, o, p, way], recv_sem=zr_sem.at[c, o, p],
            device_id=dev(me, down(1) if way else up(1)), device_id_type=MESH)

    gorder = [list(range(1, gb)) + [0], list(range(gb - 1, 0, -1)) + [0]]

    def pcopy(c, k, p, j, landed=False):
        bits = gorder[p]
        o = origin(k)
        src = wfull.at[(c, p, o) + place(bits[:j])]
        dst = wfull.at[(c, p, o) + place(bits[:j], bits[j])] if landed else src
        return pltpu.make_async_remote_copy(
            src_ref=src, dst_ref=dst,
            send_sem=ps_sem.at[c, k, p, j], recv_sem=pr_sem.at[c, k, p, j],
            device_id=dev(flip(me, 1 << bits[j]), z), device_id_type=MESH)

    def send_chunk(c):
        @pl.when(z < Z - 1)
        def _():
            for p in range(2):
                zcopy(c, z, p, 0, True).start()

        @pl.when(z > 0)
        def _():
            for p in range(2):
                zcopy(c, z, p, 1, True).start()

    def loc(c, p):
        return pltpu.make_async_copy(
            w_ref.at[(slice(None),) * (gb + 1) + (chunk_cols(c, p),)], wfull.at[c, p, z], loc_sem.at[c, p])

    for c in range(C):
        send_chunk(c)
    for c in range(C):
        for p in range(2):
            loc(c, p).start()
    for c0 in range(0, D, 256):
        tokt[c0:c0 + 256, :] = tok[:, c0:c0 + 256].T

    @pl.when(z == 0)
    def _():
        bef_buf[...] = jnp.zeros_like(bef_buf)

    @pl.when(z == Z - 1)
    def _():
        lat_buf[...] = jnp.zeros_like(lat_buf)

    for c in range(C):
        for p in range(2):
            loc(c, p).wait()

    def serve(c, k, j):
        for p in range(2):
            if j == 0:
                o = origin(k)
                zcopy(c, o, p, 0).wait_recv()

                @pl.when(jnp.logical_and(o < z, z < Z - 1))
                def _(o=o, p=p):
                    zcopy(c, o, p, 0).start()

                @pl.when(jnp.logical_and(o > z, z > 0))
                def _(o=o, p=p):
                    zcopy(c, o, p, 1).start()
            else:
                pcopy(c, k, p, j - 1, True).wait_recv()
            if j < gb:
                pcopy(c, k, p, j).start()

    def project(c):
        for p in range(2):
            prod = dot(tok[...], wfull[c, p].reshape(D, CW), 1, 0)
            kv[:, chunk_cols(c, p)] = prod.astype(BF)

    row = lax.broadcasted_iota(jnp.int32, (T, T), 0)
    col = lax.broadcasted_iota(jnp.int32, (T, T), 1)
    causal = row >= col

    def cols_of(h):
        return (pl.ds(pl.multiple_of(h * HD, HD), HD), pl.ds(pl.multiple_of(HW + h * HD, HD), HD))

    def fcopy(h):
        return pltpu.make_async_remote_copy(
            src_ref=fsnd.at[h], dst_ref=bef_buf.at[h], send_sem=fs_sem.at[h], recv_sem=fr_sem.at[h],
            device_id=dev(me, up(1)), device_id_type=MESH)

    def bcopy(h):
        return pltpu.make_async_remote_copy(
            src_ref=bsnd.at[h], dst_ref=lat_buf.at[h], send_sem=bs_sem.at[h], recv_sem=br_sem.at[h],
            device_id=dev(me, down(1)), device_id_type=MESH)

    def forward(h, _):
        hs, vs = cols_of(h)
        kf = feature(kv[:, hs].astype(F32)).astype(BF)
        qf = feature(q_ref[:, hs].astype(F32)).astype(BF)
        v = kv[:, vs]
        own = dot(kf, v, 0, 0)

        @pl.when(z > 0)
        def _():
            fcopy(h).wait_recv()

        bef = bef_buf[h]

        @pl.when(z < Z - 1)
        def _():
            fsnd[h] = (bef.astype(F32) + own).astype(BF)
            fcopy(h).start()

        sc = jnp.where(causal, dot(qf, kf, 1, 1), 0.0).astype(BF)
        sc_buf[h] = sc
        att = dot(sc, v, 1, 0) + dot(qf, bef, 1, 0)
        rinv = lax.rsqrt(jnp.mean(att * att, axis=-1, keepdims=True) + EPS)
        normed = att * rinv
        o_ref[:, hs] = normed.astype(BF)
        g = og_ref[:, hs].astype(F32)
        ga = ((g - normed * jnp.mean(g * normed, axis=-1, keepdims=True)) * rinv).astype(BF)
        ga_buf[:, hs] = ga
        og = dot(qf, ga, 0, 0)
        owng[h] = og

        @pl.when(z == Z - 1)
        def _():
            bsnd[h] = og.astype(BF)
            bcopy(h).start()

    def pass_back(h):
        @pl.when(z < Z - 1)
        def _():
            bcopy(h).wait_recv()

        @pl.when(jnp.logical_and(z > 0, z < Z - 1))
        def _():
            bsnd[h] = (lat_buf[h].astype(F32) + owng[h]).astype(BF)
            bcopy(h).start()

    def gather_lap(it, _):
        for k in range(1, Z):
            done = None
            for j in range(gb, -1, -1):
                dc = (k - 1 - j) // (Z - 1)
                kk = (k - 1 - j) % (Z - 1) + 1
                c = it + dc

                @pl.when(jnp.logical_and(c >= 0, c < C))
                def _(c=c, kk=kk, j=j):
                    serve(c, kk, j)

                if j == gb and kk == Z - 1:
                    done = c
            heads = range(k, CHUNK if k == Z - 1 else min(k + 1, CHUNK))

            @pl.when(it >= 2)
            def _(heads=heads):
                for i in heads:
                    forward((it - 2) * CHUNK + i, 0)

            @pl.when(it >= 3)
            def _(heads=heads):
                for i in heads:
                    pass_back((it - 3) * CHUNK + i - 1)

            if done is not None:
                @pl.when(jnp.logical_and(done >= 0, done < C))
                def _(c=done):
                    project(c)
                    forward(c * CHUNK, 0)

        @pl.when(it >= 3)
        def _():
            pass_back((it - 3) * CHUNK + CHUNK - 1)

        return 0

    lax.fori_loop(0, C + 2, gather_lap, 0)

    order = [list(range(nb)), [0] + list(range(nb - 1, 0, -1))]

    def slot_of(mask, bits):
        s = 0
        for j, b in enumerate(bits):
            if (mask >> b) & 1:
                s += N >> (j + 1)
        return s

    def rcopy(h, p, j):
        half = N >> (j + 1)
        return pltpu.make_async_remote_copy(
            src_ref=part.at[h, p, pl.ds(half, half)], dst_ref=rbufs[j].at[h, p],
            send_sem=rs_sem.at[h, p, j], recv_sem=rr_sem.at[h, p, j],
            device_id=dev(flip(me, 1 << order[p][j]), z), device_id_type=MESH)

    def ecopy(h, k):
        return pltpu.make_async_remote_copy(
            src_ref=fin.at[h, up(k)], dst_ref=zbuf.at[h, k],
            send_sem=es_sem.at[h, k], recv_sem=er_sem.at[h, k],
            device_id=dev(me, up(k)), device_id_type=MESH)

    rd = D // N
    rb = rd // Z

    def backward(h):
        hs, vs = cols_of(h)

        lat = lat_buf[h]
        key = kv[:, hs].astype(F32)
        kf = feature(key).astype(BF)
        qf = feature(q_ref[:, hs].astype(F32)).astype(BF)
        v = kv[:, vs]
        ga = ga_buf[:, hs]
        mw = jnp.where(causal, dot(ga, v, 1, 1), 0.0).astype(BF)
        mw_buf[h] = mw
        gk = dot(mw, qf, 0, 0) + dot(v, lat, 1, 1)
        gv = dot(sc_buf[h], ga, 0, 0) + dot(kf, lat, 1, 0)
        gkb = (gk * slope(key)).astype(BF)
        gvb = gv.astype(BF)
        kvg[:, hs] = gkb
        kvg[:, vs] = gvb
        chunk = jnp.concatenate([gkb, gvb], axis=1)
        for m in range(N):
            d = flip(me, m)
            res = dot(tokt[pl.ds(pl.multiple_of(d * rd, rd), rd), :], chunk, 1, 0) * scale
            res = res.reshape(Z, rb, 2 * HD).astype(BF)
            for p in range(2):
                part[h, p, slot_of(m, order[p])] = res[:, :, p * HD:(p + 1) * HD]
        for p in range(2):
            rcopy(h, p, 0).start()

    def stage(h, j):
        for p in range(2):
            half = N >> j
            rcopy(h, p, j - 1).wait_recv()
            if j < nb:
                part[h, p, 0:half] = part[h, p, 0:half] + rbufs[j - 1][h, p]
                rcopy(h, p, j).start()
            else:
                fin[h, :, p] = part[h, p, 0] + rbufs[j - 1][h, p, 0]
        if j == nb:
            for k in range(1, Z):
                ecopy(h, k).start()

    def finish(h):
        hs, vs = cols_of(h)
        total = fin[h, z].astype(F32)
        for k in range(1, Z):
            ecopy(h, k).wait_recv()
            total = total + zbuf[h, k].astype(F32)
        wg_ref[:, hs] = total[0]
        wg_ref[:, vs] = total[1]
        for k in range(1, Z):
            ecopy(h, k).wait_send()
        for p in range(2):
            for j in range(nb):
                rcopy(h, p, j).wait_send()

    def token_part(zz, _):
        a = jnp.zeros((T, R), F32)
        for c in range(C):
            for p in range(2):
                cols = slice(p * HW + c * CW, p * HW + (c + 1) * CW)
                a = a + dot(kvg[:, cols], wfull[c, p, zz].reshape(R, CW), 1, 1)
        tg_ref[:, pl.ds(pl.multiple_of(zz * R, 128), R)] = a.astype(BF)
        return 0

    def query_part(h, _):
        hs, vs = cols_of(h)
        kf = feature(kv[:, hs].astype(F32)).astype(BF)
        gq = dot(mw_buf[h], kf, 1, 0) + dot(ga_buf[:, hs], bef_buf[h], 1, 1)
        qg_ref[:, hs] = (gq * slope(q_ref[:, hs].astype(F32))).astype(BF)
        return 0

    def lap(it, _):
        @pl.when(it < CHUNK)
        def _():
            pass_back((C - 1) * CHUNK + it)

        @pl.when(it < HEADS)
        def _():
            backward(it)

        for j in range(1, nb + 1):
            @pl.when(jnp.logical_and(it >= j, it < HEADS + j))
            def _(j=j):
                stage(it - j, j)

        @pl.when(it >= nb + 1)
        def _():
            finish(it - nb - 1)

        @pl.when(it == HEADS)
        def _():
            lax.fori_loop(0, Z, token_part, 0)

        @pl.when(it == HEADS + 1)
        def _():
            lax.fori_loop(0, HEADS, query_part, 0)

        return 0

    lax.fori_loop(0, HEADS + nb + 1, lap, 0)

    def sent(c, _):
        for p in range(2):
            @pl.when(z < Z - 1)
            def _(p=p):
                zcopy(c, z, p, 0, True).wait_send()

            @pl.when(z > 0)
            def _(p=p):
                zcopy(c, z, p, 1, True).wait_send()

            for k in range(1, Z):
                o = origin(k)

                @pl.when(jnp.logical_and(o < z, z < Z - 1))
                def _(o=o, p=p):
                    zcopy(c, o, p, 0).wait_send()

                @pl.when(jnp.logical_and(o > z, z > 0))
                def _(o=o, p=p):
                    zcopy(c, o, p, 1).wait_send()

                for j in range(gb):
                    pcopy(c, k, p, j).wait_send()
        return 0

    lax.fori_loop(0, C, sent, 0)

    @pl.when(z < Z - 1)
    def _():
        def w(h, _):
            fcopy(h).wait_send()
            return 0
        lax.fori_loop(0, HEADS, w, 0)

    @pl.when(z > 0)
    def _():
        def w(h, _):
            bcopy(h).wait_send()
            return 0
        lax.fori_loop(0, HEADS, w, 0)


def solution(mesh):
    N = mesh.shape["dp"]
    Z = mesh.shape["seq"]

    def on_device(tokens, queries, kv_weight, out_grad):
        T, D = tokens.shape
        R = kv_weight.shape[0]
        HW = queries.shape[1]
        S = min(N, R // 16)
        r = R // S
        nb = N.bit_length() - 1
        gb = S.bit_length() - 1
        rd = D // N
        rb = rd // Z
        scale = 1.0 / math.sqrt(T * N * Z)
        vm = pl.BlockSpec(memory_space=pltpu.VMEM)
        dma = pltpu.SemaphoreType.DMA
        scratch = [
            pltpu.VMEM((HEADS // CHUNK, 2, Z) + (2,) * gb + (r, CHUNK * HD), BF),
            pltpu.VMEM((T, 2 * HW), BF),
            pltpu.VMEM((T, 2 * HW), BF),
            pltpu.VMEM((D, T), BF),
            pltpu.VMEM((T, HW), BF),
            pltpu.VMEM((HEADS, T, T), BF),
            pltpu.VMEM((HEADS, T, T), BF),
            pltpu.VMEM((HEADS, HD, HD), BF),
            pltpu.VMEM((HEADS, HD, HD), BF),
            pltpu.VMEM((HEADS, HD, HD), BF),
            pltpu.VMEM((HEADS, HD, HD), BF),
            pltpu.VMEM((HEADS, HD, HD), F32),
            pltpu.VMEM((HEADS, 2, N, Z, rb, HD), BF),
        ]
        scratch += [pltpu.VMEM((HEADS, 2, N >> (j + 1), Z, rb, HD), BF) for j in range(nb)]
        scratch += [
            pltpu.VMEM((HEADS, Z, 2, rb, HD), BF),
            pltpu.VMEM((HEADS, Z, 2, rb, HD), BF),
            dma((HEADS // CHUNK, 2)),
            dma((HEADS // CHUNK, Z, 2, 2)), dma((HEADS // CHUNK, Z, 2)),
            dma((HEADS // CHUNK, Z, 2, gb)), dma((HEADS // CHUNK, Z, 2, gb)),
            dma((HEADS,)), dma((HEADS,)),
            dma((HEADS,)), dma((HEADS,)),
            dma((HEADS, 2, nb)), dma((HEADS, 2, nb)),
            dma((HEADS, Z)), dma((HEADS, Z)),
        ]
        return pl.pallas_call(
            functools.partial(kernel, N, Z, S, scale),
            out_shape=(
                jax.ShapeDtypeStruct((T, HW), BF),
                jax.ShapeDtypeStruct((T, D), BF),
                jax.ShapeDtypeStruct((T, HW), BF),
                jax.ShapeDtypeStruct((rb, 2 * HW), F32),
            ),
            in_specs=[vm] * 4,
            out_specs=(vm,) * 4,
            scratch_shapes=scratch,
            compiler_params=pltpu.CompilerParams(
                collective_id=0, has_side_effects=True, vmem_limit_bytes=58 * 1024 * 1024
            ),
            cost_estimate=pl.CostEstimate(flops=8 * T * D * HW * 2, bytes_accessed=8 * T * D, transcendentals=T * HW * 4),
        )(tokens, queries, kv_weight.reshape((2,) * gb + (r, 2 * HW)), out_grad)

    spec = P(("dp", "seq"), None)
    return jax.shard_map(
        on_device, mesh=mesh, in_specs=(spec, spec, P("seq", None), spec),
        out_specs=(spec,) * 4, check_vma=False,
    )
```

```python
import functools
import math

import jax
import jax.numpy as jnp
from jax import lax
from jax.experimental import pallas as pl
from jax.experimental.pallas import tpu as pltpu
from jax.sharding import PartitionSpec as P

HEADS = 8
HD = 128
LAG = 4
EPS = 1e-05
MESH = pl.DeviceIdType.MESH
BF = jnp.bfloat16
F32 = jnp.float32


def dot(a, b, ca, cb):
    return lax.dot_general(a, b, (((ca,), (cb,)), ((), ())), preferred_element_type=F32)


def feature(u):
    return jnp.where(u > 0, u + 1.0, jnp.exp(jnp.minimum(u, 0.0)))


def slope(u):
    return jnp.where(u > 0, 1.0, jnp.exp(jnp.minimum(u, 0.0)))


def bit_of(x, b):
    return (x // (1 << b)) % 2


def flip(x, mask):
    b = 0
    while mask >> b:
        if (mask >> b) & 1:
            x = x + (1 << b) * (1 - 2 * bit_of(x, b))
        b += 1
    return x


def span(bits):
    masks = [0]
    for b in bits:
        masks = masks + [m | (1 << b) for m in masks]
    return masks


def kernel(
    N, Z, S, scale,
    tok, q_ref, w_ref, og_ref,
    o_ref, tg_ref, qg_ref, wg_ref,
    wfull, kvacc, kv, kvg, tokt, ga_buf, sc_buf, mw_buf, bef_buf, fsnd, lat_buf, bsnd, owng,
    part, *rest,
):
    nb = N.bit_length() - 1
    gb = S.bit_length() - 1
    rbufs = rest[:nb]
    (fin, zbuf, loc_sem, zs_sem, zr_sem, ps_sem, pr_sem, fs_sem, fr_sem, bs_sem, br_sem,
     rs_sem, rr_sem, es_sem, er_sem) = rest[nb:]
    me = lax.axis_index("dp")
    z = lax.axis_index("seq")
    T = tok.shape[0]
    D = tok.shape[1]
    HW = HEADS * HD
    R = D // Z
    sl = me % S

    def dev(dp, zz):
        return (dp, zz)

    def up(k):
        return lax.rem(z + k, Z)

    def down(k):
        return lax.rem(z + Z - k, Z)

    barrier = pltpu.get_barrier_semaphore()
    for b in range(nb):
        pl.semaphore_signal(barrier, inc=1, device_id=dev(flip(me, 1 << b), z), device_id_type=MESH)
    for k in range(1, Z):
        pl.semaphore_signal(barrier, inc=1, device_id=dev(me, up(k)), device_id_type=MESH)
    pl.semaphore_wait(barrier, nb + Z - 1)

    def origin(u):
        pairs = jnp.minimum(z, Z - 1 - z)
        near = z - (u + 1) // 2 if u % 2 else z + u // 2
        far = jnp.where(z > Z - 1 - z, z - (u - pairs), z + (u - pairs))
        return jnp.where(u <= 2 * pairs, near, far)

    def zcopy(o, p, way, own=False):
        home = wfull.at[o, p, sl]
        return pltpu.make_async_remote_copy(
            src_ref=w_ref.at[sl, :, pl.ds(p * HW, HW)] if own else home, dst_ref=home,
            send_sem=zs_sem.at[o, p, way], recv_sem=zr_sem.at[o, p],
            device_id=dev(me, down(1) if way else up(1)), device_id_type=MESH)

    def relay(o, p, wait):
        for way, cond in enumerate((jnp.logical_and(o < z, z < Z - 1), jnp.logical_and(o > z, z > 0))):
            @pl.when(cond)
            def _(way=way):
                c = zcopy(o, p, way)
                c.wait_send() if wait else c.start()

    def offer(p, wait):
        for way, cond in enumerate((z < Z - 1, z > 0)):
            @pl.when(cond)
            def _(way=way):
                c = zcopy(z, p, way, True)
                c.wait_send() if wait else c.start()

    gorder = [list(range(1, gb)) + [0], list(range(gb - 1, 0, -1)) + [0]]

    def pcopy(k, p, mask, b, landed=False):
        o = origin(k)
        s_src = flip(sl, mask | (1 << b) if landed else mask)
        return pltpu.make_async_remote_copy(
            src_ref=wfull.at[o, p, s_src], dst_ref=wfull.at[o, p, s_src],
            send_sem=ps_sem.at[k, p, mask | (1 << b)], recv_sem=pr_sem.at[k, p, mask | (1 << b)],
            device_id=dev(flip(me, 1 << b), z), device_id_type=MESH)

    def mm(o, first=False):
        t = tok[:, pl.ds(pl.multiple_of(o * R, 128), R)]
        for p in range(2):
            prod = dot(t, wfull[o, p].reshape(R, HW), 1, 0)
            cols = slice(p * HW, (p + 1) * HW)
            if first:
                kvacc[:, cols] = prod
            else:
                kvacc[:, cols] += prod

    for p in range(2):
        offer(p, False)
    loc = [pltpu.make_async_copy(w_ref.at[:, :, pl.ds(p * HW, HW)], wfull.at[z, p], loc_sem.at[p]) for p in range(2)]
    for c in loc:
        c.start()
    for c0 in range(0, D, 256):
        tokt[c0:c0 + 256, :] = tok[:, c0:c0 + 256].T

    @pl.when(z == 0)
    def _():
        bef_buf[...] = jnp.zeros_like(bef_buf)

    @pl.when(z == Z - 1)
    def _():
        lat_buf[...] = jnp.zeros_like(lat_buf)

    for c in loc:
        c.wait()
    mm(z, True)
    for t in range(Z - 1 + gb):
        for j in range(gb, -1, -1):
            k = t - j + 1
            if not 1 <= k <= Z - 1:
                continue
            for p in range(2):
                bits = gorder[p]
                if j == 0:
                    zcopy(origin(k), p, 0).wait_recv()
                    relay(origin(k), p, False)
                else:
                    for mask in span(bits[:j - 1]):
                        pcopy(k, p, mask, bits[j - 1], True).wait_recv()
                if j < gb:
                    for mask in span(bits[:j]):
                        pcopy(k, p, mask, bits[j]).start()
            if j == gb:
                mm(origin(k))
    kv[...] = kvacc[...].astype(BF)

    row = lax.broadcasted_iota(jnp.int32, (T, T), 0)
    col = lax.broadcasted_iota(jnp.int32, (T, T), 1)
    causal = row >= col

    def cols_of(h):
        return (pl.ds(pl.multiple_of(h * HD, HD), HD), pl.ds(pl.multiple_of(HW + h * HD, HD), HD))

    def fcopy(h):
        return pltpu.make_async_remote_copy(
            src_ref=fsnd.at[h], dst_ref=bef_buf.at[h], send_sem=fs_sem.at[h], recv_sem=fr_sem.at[h],
            device_id=dev(me, up(1)), device_id_type=MESH)

    def bcopy(h):
        return pltpu.make_async_remote_copy(
            src_ref=bsnd.at[h], dst_ref=lat_buf.at[h], send_sem=bs_sem.at[h], recv_sem=br_sem.at[h],
            device_id=dev(me, down(1)), device_id_type=MESH)

    def forward(h, _):
        hs, vs = cols_of(h)
        kf = feature(kv[:, hs].astype(F32)).astype(BF)
        qf = feature(q_ref[:, hs].astype(F32)).astype(BF)
        v = kv[:, vs]
        own = dot(kf, v, 0, 0)

        @pl.when(z > 0)
        def _():
            fcopy(h).wait_recv()

        bef = bef_buf[h]

        @pl.when(z < Z - 1)
        def _():
            fsnd[h] = (bef.astype(F32) + own).astype(BF)
            fcopy(h).start()

        sc = jnp.where(causal, dot(qf, kf, 1, 1), 0.0).astype(BF)
        sc_buf[h] = sc
        att = dot(sc, v, 1, 0) + dot(qf, bef, 1, 0)
        rinv = lax.rsqrt(jnp.mean(att * att, axis=-1, keepdims=True) + EPS)
        normed = att * rinv
        o_ref[:, hs] = normed.astype(BF)
        g = og_ref[:, hs].astype(F32)
        ga = ((g - normed * jnp.mean(g * normed, axis=-1, keepdims=True)) * rinv).astype(BF)
        ga_buf[:, hs] = ga
        og = dot(qf, ga, 0, 0)
        owng[h] = og

        @pl.when(z == Z - 1)
        def _():
            bsnd[h] = og.astype(BF)
            bcopy(h).start()

        @pl.when(h >= LAG)
        def _():
            pass_back(h - LAG)

        return 0

    def pass_back(h):
        @pl.when(z < Z - 1)
        def _():
            bcopy(h).wait_recv()

        @pl.when(jnp.logical_and(z > 0, z < Z - 1))
        def _():
            bsnd[h] = (lat_buf[h].astype(F32) + owng[h]).astype(BF)
            bcopy(h).start()

    lax.fori_loop(0, HEADS, forward, 0)

    order = [list(range(nb)), [0] + list(range(nb - 1, 0, -1))]

    def slot_of(mask, bits):
        s = 0
        for j, b in enumerate(bits):
            if (mask >> b) & 1:
                s += N >> (j + 1)
        return s

    def rcopy(h, p, j):
        half = N >> (j + 1)
        return pltpu.make_async_remote_copy(
            src_ref=part.at[h, p, pl.ds(half, half)], dst_ref=rbufs[j].at[h, p],
            send_sem=rs_sem.at[h, p, j], recv_sem=rr_sem.at[h, p, j],
            device_id=dev(flip(me, 1 << order[p][j]), z), device_id_type=MESH)

    def ecopy(h, k):
        return pltpu.make_async_remote_copy(
            src_ref=fin.at[h, up(k)], dst_ref=zbuf.at[h, k],
            send_sem=es_sem.at[h, k], recv_sem=er_sem.at[h, k],
            device_id=dev(me, up(k)), device_id_type=MESH)

    rd = D // N
    rb = rd // Z

    def backward(h):
        hs, vs = cols_of(h)

        lat = lat_buf[h]
        key = kv[:, hs].astype(F32)
        kf = feature(key).astype(BF)
        qf = feature(q_ref[:, hs].astype(F32)).astype(BF)
        v = kv[:, vs]
        ga = ga_buf[:, hs]
        mw = jnp.where(causal, dot(ga, v, 1, 1), 0.0).astype(BF)
        mw_buf[h] = mw
        gk = dot(mw, qf, 0, 0) + dot(v, lat, 1, 1)
        gv = dot(sc_buf[h], ga, 0, 0) + dot(kf, lat, 1, 0)
        gkb = (gk * slope(key)).astype(BF)
        gvb = gv.astype(BF)
        kvg[:, hs] = gkb
        kvg[:, vs] = gvb
        chunk = jnp.concatenate([gkb, gvb], axis=1)
        for m in range(N):
            d = flip(me, m)
            res = dot(tokt[pl.ds(pl.multiple_of(d * rd, rd), rd), :], chunk, 1, 0) * scale
            res = res.reshape(Z, rb, 2 * HD).astype(BF)
            for p in range(2):
                part[h, p, slot_of(m, order[p])] = res[:, :, p * HD:(p + 1) * HD]
        for p in range(2):
            rcopy(h, p, 0).start()

    def stage(h, j):
        for p in range(2):
            half = N >> j
            rcopy(h, p, j - 1).wait_recv()
            if j < nb:
                part[h, p, 0:half] = part[h, p, 0:half] + rbufs[j - 1][h, p]
                rcopy(h, p, j).start()
            else:
                fin[h, :, p] = part[h, p, 0] + rbufs[j - 1][h, p, 0]
        if j == nb:
            for k in range(1, Z):
                ecopy(h, k).start()

    def finish(h):
        hs, vs = cols_of(h)
        total = fin[h, z].astype(F32)
        for k in range(1, Z):
            ecopy(h, k).wait_recv()
            total = total + zbuf[h, k].astype(F32)
        wg_ref[:, hs] = total[0]
        wg_ref[:, vs] = total[1]
        for k in range(1, Z):
            ecopy(h, k).wait_send()
        for p in range(2):
            for j in range(nb):
                rcopy(h, p, j).wait_send()

    def token_part(zz, _):
        w = wfull[zz]
        a = dot(kvg[:, :HW], w[0].reshape(R, HW), 1, 1)
        a = a + dot(kvg[:, HW:], w[1].reshape(R, HW), 1, 1)
        tg_ref[:, pl.ds(pl.multiple_of(zz * R, 128), R)] = a.astype(BF)
        return 0

    def query_part(h, _):
        hs, vs = cols_of(h)
        kf = feature(kv[:, hs].astype(F32)).astype(BF)
        gq = dot(mw_buf[h], kf, 1, 0) + dot(ga_buf[:, hs], bef_buf[h], 1, 1)
        qg_ref[:, hs] = (gq * slope(q_ref[:, hs].astype(F32))).astype(BF)
        return 0

    def lap(it, _):
        @pl.when(it < LAG)
        def _():
            pass_back(HEADS - LAG + it)

        @pl.when(it < HEADS)
        def _():
            backward(it)

        for j in range(1, nb + 1):
            @pl.when(jnp.logical_and(it >= j, it < HEADS + j))
            def _(j=j):
                stage(it - j, j)

        @pl.when(it >= nb + 1)
        def _():
            finish(it - nb - 1)

        @pl.when(it == HEADS)
        def _():
            lax.fori_loop(0, Z, token_part, 0)

        @pl.when(it == HEADS + 1)
        def _():
            lax.fori_loop(0, HEADS, query_part, 0)

        return 0

    lax.fori_loop(0, HEADS + nb + 1, lap, 0)

    for p in range(2):
        offer(p, True)
    for k in range(1, Z):
        for p in range(2):
            relay(origin(k), p, True)
            bits = gorder[p]
            for j, b in enumerate(bits):
                for mask in span(bits[:j]):
                    pcopy(k, p, mask, b).wait_send()

    @pl.when(z < Z - 1)
    def _():
        def w(h, _):
            fcopy(h).wait_send()
            return 0
        lax.fori_loop(0, HEADS, w, 0)

    @pl.when(z > 0)
    def _():
        def w(h, _):
            bcopy(h).wait_send()
            return 0
        lax.fori_loop(0, HEADS, w, 0)


def solution(mesh):
    N = mesh.shape["dp"]
    Z = mesh.shape["seq"]

    def on_device(tokens, queries, kv_weight, out_grad):
        T, D = tokens.shape
        R = kv_weight.shape[0]
        HW = queries.shape[1]
        S = min(N, R // 16)
        r = R // S
        nb = N.bit_length() - 1
        rd = D // N
        rb = rd // Z
        scale = 1.0 / math.sqrt(T * N * Z)
        vm = pl.BlockSpec(memory_space=pltpu.VMEM)
        dma = pltpu.SemaphoreType.DMA
        scratch = [
            pltpu.VMEM((Z, 2, S, r, HW), BF),
            pltpu.VMEM((T, 2 * HW), F32),
            pltpu.VMEM((T, 2 * HW), BF),
            pltpu.VMEM((T, 2 * HW), BF),
            pltpu.VMEM((D, T), BF),
            pltpu.VMEM((T, HW), BF),
            pltpu.VMEM((HEADS, T, T), BF),
            pltpu.VMEM((HEADS, T, T), BF),
            pltpu.VMEM((HEADS, HD, HD), BF),
            pltpu.VMEM((HEADS, HD, HD), BF),
            pltpu.VMEM((HEADS, HD, HD), BF),
            pltpu.VMEM((HEADS, HD, HD), BF),
            pltpu.VMEM((HEADS, HD, HD), F32),
            pltpu.VMEM((HEADS, 2, N, Z, rb, HD), BF),
        ]
        scratch += [pltpu.VMEM((HEADS, 2, N >> (j + 1), Z, rb, HD), BF) for j in range(nb)]
        scratch += [
            pltpu.VMEM((HEADS, Z, 2, rb, HD), BF),
            pltpu.VMEM((HEADS, Z, 2, rb, HD), BF),
            dma((2,)),
            dma((Z, 2, 2)), dma((Z, 2)),
            dma((Z, 2, S)), dma((Z, 2, S)),
            dma((HEADS,)), dma((HEADS,)),
            dma((HEADS,)), dma((HEADS,)),
            dma((HEADS, 2, nb)), dma((HEADS, 2, nb)),
            dma((HEADS, Z)), dma((HEADS, Z)),
        ]
        return pl.pallas_call(
            functools.partial(kernel, N, Z, S, scale),
            out_shape=(
                jax.ShapeDtypeStruct((T, HW), BF),
                jax.ShapeDtypeStruct((T, D), BF),
                jax.ShapeDtypeStruct((T, HW), BF),
                jax.ShapeDtypeStruct((rb, 2 * HW), F32),
            ),
            in_specs=[vm] * 4,
            out_specs=(vm,) * 4,
            scratch_shapes=scratch,
            compiler_params=pltpu.CompilerParams(
                collective_id=0, has_side_effects=True, vmem_limit_bytes=58 * 1024 * 1024
            ),
            cost_estimate=pl.CostEstimate(flops=8 * T * D * HW * 2, bytes_accessed=8 * T * D, transcendentals=T * HW * 4),
        )(tokens, queries, kv_weight.reshape(S, r, 2 * HW), out_grad)

    spec = P(("dp", "seq"), None)
    return jax.shard_map(
        on_device, mesh=mesh, in_specs=(spec, spec, P("seq", None), spec),
        out_specs=(spec,) * 4, check_vma=False,
    )
```

```python
import functools
import math

import jax
import jax.numpy as jnp
from jax import lax
from jax.experimental import pallas as pl
from jax.experimental.pallas import tpu as pltpu
from jax.sharding import PartitionSpec as P

HEADS = 8
HD = 128
CHUNK = 4
EPS = 1e-05
MESH = pl.DeviceIdType.MESH
BF = jnp.bfloat16
F32 = jnp.float32


def dot(a, b, ca, cb):
    return lax.dot_general(a, b, (((ca,), (cb,)), ((), ())), preferred_element_type=F32)


def feature(u):
    return jnp.where(u > 0, u + 1.0, jnp.exp(jnp.minimum(u, 0.0)))


def slope(u):
    return jnp.where(u > 0, 1.0, jnp.exp(jnp.minimum(u, 0.0)))


def bit_of(x, b):
    return (x // (1 << b)) % 2


def flip(x, mask):
    b = 0
    while mask >> b:
        if (mask >> b) & 1:
            x = x + (1 << b) * (1 - 2 * bit_of(x, b))
        b += 1
    return x


def kernel(
    N, Z, S, scale,
    tok, q_ref, w_ref, og_ref,
    o_ref, tg_ref, qg_ref, wg_ref,
    wfull, kv, kvg, tokt, ga_buf, sc_buf, mw_buf, bef_buf, fsnd, lat_buf, bsnd, owng,
    part, *rest,
):
    nb = N.bit_length() - 1
    gb = S.bit_length() - 1
    rbufs = rest[:nb]
    (fin, zbuf, loc_sem, zs_sem, zr_sem, ps_sem, pr_sem, fs_sem, fr_sem, bs_sem, br_sem,
     rs_sem, rr_sem, es_sem, er_sem) = rest[nb:]
    me = lax.axis_index("dp")
    z = lax.axis_index("seq")
    T = tok.shape[0]
    D = tok.shape[1]
    HW = HEADS * HD
    R = D // Z
    sl = me % S

    def dev(dp, zz):
        return (dp, zz)

    def up(k):
        return lax.rem(z + k, Z)

    def down(k):
        return lax.rem(z + Z - k, Z)

    barrier = pltpu.get_barrier_semaphore()
    for b in range(nb):
        pl.semaphore_signal(barrier, inc=1, device_id=dev(flip(me, 1 << b), z), device_id_type=MESH)
    for k in range(1, Z):
        pl.semaphore_signal(barrier, inc=1, device_id=dev(me, up(k)), device_id_type=MESH)
    pl.semaphore_wait(barrier, nb + Z - 1)

    CW = CHUNK * HD
    C = HEADS // CHUNK

    def place(spread, flipped=None):
        at = []
        for b in reversed(range(gb)):
            if b in spread:
                at.append(slice(None))
            else:
                at.append(1 - bit_of(sl, b) if b == flipped else bit_of(sl, b))
        return tuple(at)

    def chunk_cols(c, p):
        return pl.ds(pl.multiple_of(p * HW + c * CW, CW), CW)

    def origin(u):
        pairs = jnp.minimum(z, Z - 1 - z)
        near = z - (u + 1) // 2 if u % 2 else z + u // 2
        far = jnp.where(z > Z - 1 - z, z - (u - pairs), z + (u - pairs))
        return jnp.where(u <= 2 * pairs, near, far)

    def zcopy(c, o, p, way, own=False):
        home = wfull.at[(c, p, o) + place(())]
        src = w_ref.at[place(()) + (slice(None), chunk_cols(c, p))] if own else home
        return pltpu.make_async_remote_copy(
            src_ref=src, dst_ref=home,
            send_sem=zs_sem.at[c, o, p, way], recv_sem=zr_sem.at[c, o, p],
            device_id=dev(me, down(1) if way else up(1)), device_id_type=MESH)

    gorder = [list(range(1, gb)) + [0], list(range(gb - 1, 0, -1)) + [0]]

    def pcopy(c, k, p, j, landed=False):
        bits = gorder[p]
        o = origin(k)
        src = wfull.at[(c, p, o) + place(bits[:j])]
        dst = wfull.at[(c, p, o) + place(bits[:j], bits[j])] if landed else src
        return pltpu.make_async_remote_copy(
            src_ref=src, dst_ref=dst,
            send_sem=ps_sem.at[c, k, p, j], recv_sem=pr_sem.at[c, k, p, j],
            device_id=dev(flip(me, 1 << bits[j]), z), device_id_type=MESH)

    def send_chunk(c):
        @pl.when(z < Z - 1)
        def _():
            for p in range(2):
                zcopy(c, z, p, 0, True).start()

        @pl.when(z > 0)
        def _():
            for p in range(2):
                zcopy(c, z, p, 1, True).start()

    def loc(c, p):
        return pltpu.make_async_copy(
            w_ref.at[(slice(None),) * (gb + 1) + (chunk_cols(c, p),)], wfull.at[c, p, z], loc_sem.at[c, p])

    for c in range(C):
        send_chunk(c)
    for c in range(C):
        for p in range(2):
            loc(c, p).start()
    for c0 in range(0, D, 256):
        tokt[c0:c0 + 256, :] = tok[:, c0:c0 + 256].T

    @pl.when(z == 0)
    def _():
        bef_buf[...] = jnp.zeros_like(bef_buf)

    @pl.when(z == Z - 1)
    def _():
        lat_buf[...] = jnp.zeros_like(lat_buf)

    for c in range(C):
        for p in range(2):
            loc(c, p).wait()

    def serve(c, k, j):
        for p in range(2):
            if j == 0:
                o = origin(k)
                zcopy(c, o, p, 0).wait_recv()

                @pl.when(jnp.logical_and(o < z, z < Z - 1))
                def _(o=o, p=p):
                    zcopy(c, o, p, 0).start()

                @pl.when(jnp.logical_and(o > z, z > 0))
                def _(o=o, p=p):
                    zcopy(c, o, p, 1).start()
            else:
                pcopy(c, k, p, j - 1, True).wait_recv()
            if j < gb:
                pcopy(c, k, p, j).start()

    def project(c):
        for p in range(2):
            prod = dot(tok[...], wfull[c, p].reshape(D, CW), 1, 0)
            kv[:, chunk_cols(c, p)] = prod.astype(BF)

    row = lax.broadcasted_iota(jnp.int32, (T, T), 0)
    col = lax.broadcasted_iota(jnp.int32, (T, T), 1)
    causal = row >= col

    def cols_of(h):
        return (pl.ds(pl.multiple_of(h * HD, HD), HD), pl.ds(pl.multiple_of(HW + h * HD, HD), HD))

    def fcopy(h):
        return pltpu.make_async_remote_copy(
            src_ref=fsnd.at[h], dst_ref=bef_buf.at[h], send_sem=fs_sem.at[h], recv_sem=fr_sem.at[h],
            device_id=dev(me, up(1)), device_id_type=MESH)

    def bcopy(h):
        return pltpu.make_async_remote_copy(
            src_ref=bsnd.at[h], dst_ref=lat_buf.at[h], send_sem=bs_sem.at[h], recv_sem=br_sem.at[h],
            device_id=dev(me, down(1)), device_id_type=MESH)

    def forward(h, _):
        hs, vs = cols_of(h)
        kf = feature(kv[:, hs].astype(F32)).astype(BF)
        qf = feature(q_ref[:, hs].astype(F32)).astype(BF)
        v = kv[:, vs]
        own = dot(kf, v, 0, 0)

        @pl.when(z > 0)
        def _():
            fcopy(h).wait_recv()

        bef = bef_buf[h]

        @pl.when(z < Z - 1)
        def _():
            fsnd[h] = (bef.astype(F32) + own).astype(BF)
            fcopy(h).start()

        sc = jnp.where(causal, dot(qf, kf, 1, 1), 0.0).astype(BF)
        sc_buf[h] = sc
        att = dot(sc, v, 1, 0) + dot(qf, bef, 1, 0)
        rinv = lax.rsqrt(jnp.mean(att * att, axis=-1, keepdims=True) + EPS)
        normed = att * rinv
        o_ref[:, hs] = normed.astype(BF)
        g = og_ref[:, hs].astype(F32)
        ga = ((g - normed * jnp.mean(g * normed, axis=-1, keepdims=True)) * rinv).astype(BF)
        ga_buf[:, hs] = ga
        og = dot(qf, ga, 0, 0)
        owng[h] = og

        @pl.when(z == Z - 1)
        def _():
            bsnd[h] = og.astype(BF)
            bcopy(h).start()

    def pass_back(h):
        @pl.when(z < Z - 1)
        def _():
            bcopy(h).wait_recv()

        @pl.when(jnp.logical_and(z > 0, z < Z - 1))
        def _():
            bsnd[h] = (lat_buf[h].astype(F32) + owng[h]).astype(BF)
            bcopy(h).start()

    def gather_lap(it, _):
        for k in range(1, Z):
            done = None
            for j in range(gb, -1, -1):
                dc = (k - 1 - j) // (Z - 1)
                kk = (k - 1 - j) % (Z - 1) + 1
                c = it + dc

                @pl.when(jnp.logical_and(c >= 0, c < C))
                def _(c=c, kk=kk, j=j):
                    serve(c, kk, j)

                if j == gb and kk == Z - 1:
                    done = c
            heads = range(k, CHUNK if k == Z - 1 else min(k + 1, CHUNK))

            @pl.when(it >= 2)
            def _(heads=heads):
                for i in heads:
                    forward((it - 2) * CHUNK + i, 0)

            if done is not None:
                @pl.when(jnp.logical_and(done >= 0, done < C))
                def _(c=done):
                    project(c)
                    forward(c * CHUNK, 0)

        return 0

    lax.fori_loop(0, C + 2, gather_lap, 0)

    order = [list(range(nb)), [0] + list(range(nb - 1, 0, -1))]

    def slot_of(mask, bits):
        s = 0
        for j, b in enumerate(bits):
            if (mask >> b) & 1:
                s += N >> (j + 1)
        return s

    def rcopy(h, p, j):
        half = N >> (j + 1)
        return pltpu.make_async_remote_copy(
            src_ref=part.at[h, p, pl.ds(half, half)], dst_ref=rbufs[j].at[h, p],
            send_sem=rs_sem.at[h, p, j], recv_sem=rr_sem.at[h, p, j],
            device_id=dev(flip(me, 1 << order[p][j]), z), device_id_type=MESH)

    def ecopy(h, k):
        return pltpu.make_async_remote_copy(
            src_ref=fin.at[h, up(k)], dst_ref=zbuf.at[h, k],
            send_sem=es_sem.at[h, k], recv_sem=er_sem.at[h, k],
            device_id=dev(me, up(k)), device_id_type=MESH)

    rd = D // N
    rb = rd // Z

    def backward(h):
        hs, vs = cols_of(h)

        lat = lat_buf[h]
        key = kv[:, hs].astype(F32)
        kf = feature(key).astype(BF)
        qf = feature(q_ref[:, hs].astype(F32)).astype(BF)
        v = kv[:, vs]
        ga = ga_buf[:, hs]
        mw = jnp.where(causal, dot(ga, v, 1, 1), 0.0).astype(BF)
        mw_buf[h] = mw
        gk = dot(mw, qf, 0, 0) + dot(v, lat, 1, 1)
        gv = dot(sc_buf[h], ga, 0, 0) + dot(kf, lat, 1, 0)
        gkb = (gk * slope(key)).astype(BF)
        gvb = gv.astype(BF)
        kvg[:, hs] = gkb
        kvg[:, vs] = gvb
        chunk = jnp.concatenate([gkb, gvb], axis=1)
        for m in range(N):
            d = flip(me, m)
            res = dot(tokt[pl.ds(pl.multiple_of(d * rd, rd), rd), :], chunk, 1, 0) * scale
            res = res.reshape(Z, rb, 2 * HD).astype(BF)
            for p in range(2):
                part[h, p, slot_of(m, order[p])] = res[:, :, p * HD:(p + 1) * HD]
        for p in range(2):
            rcopy(h, p, 0).start()

    def stage(h, j):
        for p in range(2):
            half = N >> j
            rcopy(h, p, j - 1).wait_recv()
            if j < nb:
                part[h, p, 0:half] = part[h, p, 0:half] + rbufs[j - 1][h, p]
                rcopy(h, p, j).start()
            else:
                fin[h, :, p] = part[h, p, 0] + rbufs[j - 1][h, p, 0]
        if j == nb:
            for k in range(1, Z):
                ecopy(h, k).start()

    def finish(h):
        hs, vs = cols_of(h)
        total = fin[h, z].astype(F32)
        for k in range(1, Z):
            ecopy(h, k).wait_recv()
            total = total + zbuf[h, k].astype(F32)
        wg_ref[:, hs] = total[0]
        wg_ref[:, vs] = total[1]
        for k in range(1, Z):
            ecopy(h, k).wait_send()
        for p in range(2):
            for j in range(nb):
                rcopy(h, p, j).wait_send()

    def token_part(zz, _):
        a = jnp.zeros((T, R), F32)
        for c in range(C):
            for p in range(2):
                cols = slice(p * HW + c * CW, p * HW + (c + 1) * CW)
                a = a + dot(kvg[:, cols], wfull[c, p, zz].reshape(R, CW), 1, 1)
        tg_ref[:, pl.ds(pl.multiple_of(zz * R, 128), R)] = a.astype(BF)
        return 0

    def query_part(h, _):
        hs, vs = cols_of(h)
        kf = feature(kv[:, hs].astype(F32)).astype(BF)
        gq = dot(mw_buf[h], kf, 1, 0) + dot(ga_buf[:, hs], bef_buf[h], 1, 1)
        qg_ref[:, hs] = (gq * slope(q_ref[:, hs].astype(F32))).astype(BF)
        return 0

    def lap(it, _):
        @pl.when(it < HEADS)
        def _():
            pass_back(it)
            backward(it)

        for j in range(1, nb + 1):
            @pl.when(jnp.logical_and(it >= j, it < HEADS + j))
            def _(j=j):
                stage(it - j, j)

        @pl.when(it >= nb + 1)
        def _():
            finish(it - nb - 1)

        @pl.when(it == HEADS)
        def _():
            lax.fori_loop(0, Z, token_part, 0)

        @pl.when(it == HEADS + 1)
        def _():
            lax.fori_loop(0, HEADS, query_part, 0)

        return 0

    lax.fori_loop(0, HEADS + nb + 1, lap, 0)

    def sent(c, _):
        for p in range(2):
            @pl.when(z < Z - 1)
            def _(p=p):
                zcopy(c, z, p, 0, True).wait_send()

            @pl.when(z > 0)
            def _(p=p):
                zcopy(c, z, p, 1, True).wait_send()

            for k in range(1, Z):
                o = origin(k)

                @pl.when(jnp.logical_and(o < z, z < Z - 1))
                def _(o=o, p=p):
                    zcopy(c, o, p, 0).wait_send()

                @pl.when(jnp.logical_and(o > z, z > 0))
                def _(o=o, p=p):
                    zcopy(c, o, p, 1).wait_send()

                for j in range(gb):
                    pcopy(c, k, p, j).wait_send()
        return 0

    lax.fori_loop(0, C, sent, 0)

    @pl.when(z < Z - 1)
    def _():
        def w(h, _):
            fcopy(h).wait_send()
            return 0
        lax.fori_loop(0, HEADS, w, 0)

    @pl.when(z > 0)
    def _():
        def w(h, _):
            bcopy(h).wait_send()
            return 0
        lax.fori_loop(0, HEADS, w, 0)


def solution(mesh):
    N = mesh.shape["dp"]
    Z = mesh.shape["seq"]

    def on_device(tokens, queries, kv_weight, out_grad):
        T, D = tokens.shape
        R = kv_weight.shape[0]
        HW = queries.shape[1]
        S = min(N, R // 16)
        r = R // S
        nb = N.bit_length() - 1
        gb = S.bit_length() - 1
        rd = D // N
        rb = rd // Z
        scale = 1.0 / math.sqrt(T * N * Z)
        vm = pl.BlockSpec(memory_space=pltpu.VMEM)
        dma = pltpu.SemaphoreType.DMA
        scratch = [
            pltpu.VMEM((HEADS // CHUNK, 2, Z) + (2,) * gb + (r, CHUNK * HD), BF),
            pltpu.VMEM((T, 2 * HW), BF),
            pltpu.VMEM((T, 2 * HW), BF),
            pltpu.VMEM((D, T), BF),
            pltpu.VMEM((T, HW), BF),
            pltpu.VMEM((HEADS, T, T), BF),
            pltpu.VMEM((HEADS, T, T), BF),
            pltpu.VMEM((HEADS, HD, HD), BF),
            pltpu.VMEM((HEADS, HD, HD), BF),
            pltpu.VMEM((HEADS, HD, HD), BF),
            pltpu.VMEM((HEADS, HD, HD), BF),
            pltpu.VMEM((HEADS, HD, HD), F32),
            pltpu.VMEM((HEADS, 2, N, Z, rb, HD), BF),
        ]
        scratch += [pltpu.VMEM((HEADS, 2, N >> (j + 1), Z, rb, HD), BF) for j in range(nb)]
        scratch += [
            pltpu.VMEM((HEADS, Z, 2, rb, HD), BF),
            pltpu.VMEM((HEADS, Z, 2, rb, HD), BF),
            dma((HEADS // CHUNK, 2)),
            dma((HEADS // CHUNK, Z, 2, 2)), dma((HEADS // CHUNK, Z, 2)),
            dma((HEADS // CHUNK, Z, 2, gb)), dma((HEADS // CHUNK, Z, 2, gb)),
            dma((HEADS,)), dma((HEADS,)),
            dma((HEADS,)), dma((HEADS,)),
            dma((HEADS, 2, nb)), dma((HEADS, 2, nb)),
            dma((HEADS, Z)), dma((HEADS, Z)),
        ]
        return pl.pallas_call(
            functools.partial(kernel, N, Z, S, scale),
            out_shape=(
                jax.ShapeDtypeStruct((T, HW), BF),
                jax.ShapeDtypeStruct((T, D), BF),
                jax.ShapeDtypeStruct((T, HW), BF),
                jax.ShapeDtypeStruct((rb, 2 * HW), F32),
            ),
            in_specs=[vm] * 4,
            out_specs=(vm,) * 4,
            scratch_shapes=scratch,
            compiler_params=pltpu.CompilerParams(
                collective_id=0, has_side_effects=True, vmem_limit_bytes=58 * 1024 * 1024
            ),
            cost_estimate=pl.CostEstimate(flops=8 * T * D * HW * 2, bytes_accessed=8 * T * D, transcendentals=T * HW * 4),
        )(tokens, queries, kv_weight.reshape((2,) * gb + (r, 2 * HW)), out_grad)

    spec = P(("dp", "seq"), None)
    return jax.shard_map(
        on_device, mesh=mesh, in_specs=(spec, spec, P("seq", None), spec),
        out_specs=(spec,) * 4, check_vma=False,
    )
```

```python
import functools
import math

import jax
import jax.numpy as jnp
from jax import lax
from jax.experimental import pallas as pl
from jax.experimental.pallas import tpu as pltpu
from jax.sharding import PartitionSpec as P

HEADS = 8
HD = 128
PAIR = 2
EPS = 1e-05
MESH = pl.DeviceIdType.MESH
BF = jnp.bfloat16
F32 = jnp.float32


def dot(a, b, ca, cb):
    return lax.dot_general(a, b, (((ca,), (cb,)), ((), ())), preferred_element_type=F32)


def feature(u):
    return jnp.where(u > 0, u + 1.0, jnp.exp(jnp.minimum(u, 0.0)))


def slope(u):
    return jnp.where(u > 0, 1.0, jnp.exp(jnp.minimum(u, 0.0)))


def bit_of(x, b):
    return (x // (1 << b)) % 2


def flip(x, mask):
    b = 0
    while mask >> b:
        if (mask >> b) & 1:
            x = x + (1 << b) * (1 - 2 * bit_of(x, b))
        b += 1
    return x


def span(bits):
    masks = [0]
    for b in bits:
        masks = masks + [m | (1 << b) for m in masks]
    return masks


def kernel(
    N, Z, S, scale,
    tok, q_ref, w_ref, og_ref,
    o_ref, tg_ref, qg_ref, wg_ref,
    wfull, kvacc, kv, kvg, tokt, ga_buf, sc_buf, mw_buf, bef_buf, fsnd, lat_buf, bsnd, owng,
    part, *rest,
):
    nb = N.bit_length() - 1
    gb = S.bit_length() - 1
    rbufs = rest[:nb]
    (fin, zbuf, loc_sem, zs_sem, zr_sem, ps_sem, pr_sem, fs_sem, fr_sem, bs_sem, br_sem,
     rs_sem, rr_sem, es_sem, er_sem) = rest[nb:]
    me = lax.axis_index("dp")
    z = lax.axis_index("seq")
    T = tok.shape[0]
    D = tok.shape[1]
    HW = HEADS * HD
    R = D // Z
    sl = me % S

    def dev(dp, zz):
        return (dp, zz)

    def up(k):
        return lax.rem(z + k, Z)

    def down(k):
        return lax.rem(z + Z - k, Z)

    barrier = pltpu.get_barrier_semaphore()
    for b in range(nb):
        pl.semaphore_signal(barrier, inc=1, device_id=dev(flip(me, 1 << b), z), device_id_type=MESH)
    for k in range(1, Z):
        pl.semaphore_signal(barrier, inc=1, device_id=dev(me, up(k)), device_id_type=MESH)
    pl.semaphore_wait(barrier, nb + Z - 1)

    def origin(u):
        pairs = jnp.minimum(z, Z - 1 - z)
        near = z - (u + 1) // 2 if u % 2 else z + u // 2
        far = jnp.where(z > Z - 1 - z, z - (u - pairs), z + (u - pairs))
        return jnp.where(u <= 2 * pairs, near, far)

    def zcopy(u, p, landed=False):
        o = origin(u) if landed else z
        return pltpu.make_async_remote_copy(
            src_ref=w_ref.at[sl, :, pl.ds(p * HW, HW)], dst_ref=wfull.at[o, p, sl],
            send_sem=zs_sem.at[u, p], recv_sem=zr_sem.at[o, p],
            device_id=dev(me, origin(u)), device_id_type=MESH)

    gorder = [list(range(1, gb)) + [0], list(range(gb - 1, 0, -1)) + [0]]

    def pcopy(k, p, mask, b, landed=False):
        o = origin(k)
        s_src = flip(sl, mask | (1 << b) if landed else mask)
        return pltpu.make_async_remote_copy(
            src_ref=wfull.at[o, p, s_src], dst_ref=wfull.at[o, p, s_src],
            send_sem=ps_sem.at[k, p, mask | (1 << b)], recv_sem=pr_sem.at[k, p, mask | (1 << b)],
            device_id=dev(flip(me, 1 << b), z), device_id_type=MESH)

    def mm(o, first=False):
        t = tok[:, pl.ds(pl.multiple_of(o * R, 128), R)]
        for p in range(2):
            prod = dot(t, wfull[o, p].reshape(R, HW), 1, 0)
            cols = slice(p * HW, (p + 1) * HW)
            if first:
                kvacc[:, cols] = prod
            else:
                kvacc[:, cols] += prod

    for k in range(1, Z):
        for p in range(2):
            zcopy(k, p).start()
    loc = [pltpu.make_async_copy(w_ref.at[:, :, pl.ds(p * HW, HW)], wfull.at[z, p], loc_sem.at[p]) for p in range(2)]
    for c in loc:
        c.start()
    for c0 in range(0, D, 256):
        tokt[c0:c0 + 256, :] = tok[:, c0:c0 + 256].T

    @pl.when(z == 0)
    def _():
        bef_buf[...] = jnp.zeros_like(bef_buf)

    @pl.when(z == Z - 1)
    def _():
        lat_buf[...] = jnp.zeros_like(lat_buf)

    for c in loc:
        c.wait()
    mm(z, True)
    for t in range(Z - 1 + gb):
        for j in range(gb, -1, -1):
            k = t - j + 1
            if not 1 <= k <= Z - 1:
                continue
            for p in range(2):
                bits = gorder[p]
                if j == 0:
                    zcopy(k, p, True).wait_recv()
                else:
                    for mask in span(bits[:j - 1]):
                        pcopy(k, p, mask, bits[j - 1], True).wait_recv()
                if j < gb:
                    for mask in span(bits[:j]):
                        pcopy(k, p, mask, bits[j]).start()
            if j == gb:
                mm(origin(k))
    kv[...] = kvacc[...].astype(BF)

    row = lax.broadcasted_iota(jnp.int32, (T, T), 0)
    col = lax.broadcasted_iota(jnp.int32, (T, T), 1)
    causal = row >= col

    def cols_of(h):
        return (pl.ds(pl.multiple_of(h * HD, HD), HD), pl.ds(pl.multiple_of(HW + h * HD, HD), HD))

    def fcopy(h):
        return pltpu.make_async_remote_copy(
            src_ref=fsnd.at[h], dst_ref=bef_buf.at[h], send_sem=fs_sem.at[h], recv_sem=fr_sem.at[h],
            device_id=dev(me, up(1)), device_id_type=MESH)

    def bcopy(h):
        return pltpu.make_async_remote_copy(
            src_ref=bsnd.at[h], dst_ref=lat_buf.at[h], send_sem=bs_sem.at[h], recv_sem=br_sem.at[h],
            device_id=dev(me, down(1)), device_id_type=MESH)

    def forward(i, _):
        heads = [i * PAIR + n for n in range(PAIR)]
        kfs, qfs, vs_, owns = [], [], [], []
        for h in heads:
            hs, vs = cols_of(h)
            kf = feature(kv[:, hs].astype(F32)).astype(BF)
            v = kv[:, vs]
            kfs.append(kf)
            qfs.append(feature(q_ref[:, hs].astype(F32)).astype(BF))
            vs_.append(v)
            owns.append(dot(kf, v, 0, 0))

        @pl.when(z > 0)
        def _():
            for h in heads:
                fcopy(h).wait_recv()

        @pl.when(z < Z - 1)
        def _():
            for h, own in zip(heads, owns):
                fsnd[h] = (bef_buf[h].astype(F32) + own).astype(BF)
                fcopy(h).start()

        scs = [jnp.where(causal, dot(qf, kf, 1, 1), 0.0).astype(BF) for qf, kf in zip(qfs, kfs)]
        atts = [dot(sc, v, 1, 0) + dot(qf, bef_buf[h], 1, 0) for sc, v, qf, h in zip(scs, vs_, qfs, heads)]
        rinvs = [lax.rsqrt(jnp.mean(att * att, axis=-1, keepdims=True) + EPS) for att in atts]
        for h, sc, att, rinv, qf in zip(heads, scs, atts, rinvs, qfs):
            hs, vs = cols_of(h)
            sc_buf[h] = sc
            normed = att * rinv
            o_ref[:, hs] = normed.astype(BF)
            g = og_ref[:, hs].astype(F32)
            ga = ((g - normed * jnp.mean(g * normed, axis=-1, keepdims=True)) * rinv).astype(BF)
            ga_buf[:, hs] = ga
            owng[h] = dot(qf, ga, 0, 0)

        @pl.when(z == Z - 1)
        def _():
            for h in heads:
                bsnd[h] = owng[h].astype(BF)
                bcopy(h).start()

        return 0

    lax.fori_loop(0, HEADS // PAIR, forward, 0)

    order = [list(range(nb)), [0] + list(range(nb - 1, 0, -1))]

    def slot_of(mask, bits):
        s = 0
        for j, b in enumerate(bits):
            if (mask >> b) & 1:
                s += N >> (j + 1)
        return s

    def rcopy(h, p, j):
        half = N >> (j + 1)
        return pltpu.make_async_remote_copy(
            src_ref=part.at[h, p, pl.ds(half, half)], dst_ref=rbufs[j].at[h, p],
            send_sem=rs_sem.at[h, p, j], recv_sem=rr_sem.at[h, p, j],
            device_id=dev(flip(me, 1 << order[p][j]), z), device_id_type=MESH)

    def ecopy(h, k):
        return pltpu.make_async_remote_copy(
            src_ref=fin.at[h, up(k)], dst_ref=zbuf.at[h, k],
            send_sem=es_sem.at[h, k], recv_sem=er_sem.at[h, k],
            device_id=dev(me, up(k)), device_id_type=MESH)

    rd = D // N
    rb = rd // Z

    def backward(h):
        hs, vs = cols_of(h)

        @pl.when(z < Z - 1)
        def _():
            bcopy(h).wait_recv()

        lat = lat_buf[h]

        @pl.when(jnp.logical_and(z > 0, z < Z - 1))
        def _():
            bsnd[h] = (lat.astype(F32) + owng[h]).astype(BF)
            bcopy(h).start()

        key = kv[:, hs].astype(F32)
        kf = feature(key).astype(BF)
        qf = feature(q_ref[:, hs].astype(F32)).astype(BF)
        v = kv[:, vs]
        ga = ga_buf[:, hs]
        mw = jnp.where(causal, dot(ga, v, 1, 1), 0.0).astype(BF)
        mw_buf[h] = mw
        gk = dot(mw, qf, 0, 0) + dot(v, lat, 1, 1)
        gv = dot(sc_buf[h], ga, 0, 0) + dot(kf, lat, 1, 0)
        gkb = (gk * slope(key)).astype(BF)
        gvb = gv.astype(BF)
        kvg[:, hs] = gkb
        kvg[:, vs] = gvb
        chunk = jnp.concatenate([gkb, gvb], axis=1)
        for m in range(N):
            d = flip(me, m)
            res = dot(tokt[pl.ds(pl.multiple_of(d * rd, rd), rd), :], chunk, 1, 0) * scale
            res = res.reshape(Z, rb, 2 * HD).astype(BF)
            for p in range(2):
                part[h, p, slot_of(m, order[p])] = res[:, :, p * HD:(p + 1) * HD]
        for p in range(2):
            rcopy(h, p, 0).start()

    def stage(h, j):
        for p in range(2):
            half = N >> j
            rcopy(h, p, j - 1).wait_recv()
            if j < nb:
                part[h, p, 0:half] = part[h, p, 0:half] + rbufs[j - 1][h, p]
                rcopy(h, p, j).start()
            else:
                fin[h, :, p] = part[h, p, 0] + rbufs[j - 1][h, p, 0]
        if j == nb:
            for k in range(1, Z):
                ecopy(h, k).start()

    def finish(h):
        hs, vs = cols_of(h)
        total = fin[h, z].astype(F32)
        for k in range(1, Z):
            ecopy(h, k).wait_recv()
            total = total + zbuf[h, k].astype(F32)
        wg_ref[:, hs] = total[0]
        wg_ref[:, vs] = total[1]
        for k in range(1, Z):
            ecopy(h, k).wait_send()
        for p in range(2):
            for j in range(nb):
                rcopy(h, p, j).wait_send()

    def token_part(zz, _):
        w = wfull[zz]
        a = dot(kvg[:, :HW], w[0].reshape(R, HW), 1, 1)
        a = a + dot(kvg[:, HW:], w[1].reshape(R, HW), 1, 1)
        tg_ref[:, pl.ds(pl.multiple_of(zz * R, 128), R)] = a.astype(BF)
        return 0

    def query_part(h, _):
        hs, vs = cols_of(h)
        kf = feature(kv[:, hs].astype(F32)).astype(BF)
        gq = dot(mw_buf[h], kf, 1, 0) + dot(ga_buf[:, hs], bef_buf[h], 1, 1)
        qg_ref[:, hs] = (gq * slope(q_ref[:, hs].astype(F32))).astype(BF)
        return 0

    def lap(it, _):
        @pl.when(it < HEADS)
        def _():
            backward(it)

        for j in range(1, nb + 1):
            @pl.when(jnp.logical_and(it >= j, it < HEADS + j))
            def _(j=j):
                stage(it - j, j)

        @pl.when(it >= nb + 1)
        def _():
            finish(it - nb - 1)

        @pl.when(it == HEADS)
        def _():
            lax.fori_loop(0, Z, token_part, 0)

        @pl.when(it == HEADS + 1)
        def _():
            lax.fori_loop(0, HEADS, query_part, 0)

        return 0

    lax.fori_loop(0, HEADS + nb + 1, lap, 0)

    for k in range(1, Z):
        for p in range(2):
            zcopy(k, p).wait_send()
            bits = gorder[p]
            for j, b in enumerate(bits):
                for mask in span(bits[:j]):
                    pcopy(k, p, mask, b).wait_send()

    @pl.when(z < Z - 1)
    def _():
        def w(h, _):
            fcopy(h).wait_send()
            return 0
        lax.fori_loop(0, HEADS, w, 0)

    @pl.when(z > 0)
    def _():
        def w(h, _):
            bcopy(h).wait_send()
            return 0
        lax.fori_loop(0, HEADS, w, 0)


def solution(mesh):
    N = mesh.shape["dp"]
    Z = mesh.shape["seq"]

    def on_device(tokens, queries, kv_weight, out_grad):
        T, D = tokens.shape
        R = kv_weight.shape[0]
        HW = queries.shape[1]
        S = min(N, R // 16)
        r = R // S
        nb = N.bit_length() - 1
        rd = D // N
        rb = rd // Z
        scale = 1.0 / math.sqrt(T * N * Z)
        vm = pl.BlockSpec(memory_space=pltpu.VMEM)
        dma = pltpu.SemaphoreType.DMA
        scratch = [
            pltpu.VMEM((Z, 2, S, r, HW), BF),
            pltpu.VMEM((T, 2 * HW), F32),
            pltpu.VMEM((T, 2 * HW), BF),
            pltpu.VMEM((T, 2 * HW), BF),
            pltpu.VMEM((D, T), BF),
            pltpu.VMEM((T, HW), BF),
            pltpu.VMEM((HEADS, T, T), BF),
            pltpu.VMEM((HEADS, T, T), BF),
            pltpu.VMEM((HEADS, HD, HD), BF),
            pltpu.VMEM((HEADS, HD, HD), BF),
            pltpu.VMEM((HEADS, HD, HD), BF),
            pltpu.VMEM((HEADS, HD, HD), BF),
            pltpu.VMEM((HEADS, HD, HD), F32),
            pltpu.VMEM((HEADS, 2, N, Z, rb, HD), BF),
        ]
        scratch += [pltpu.VMEM((HEADS, 2, N >> (j + 1), Z, rb, HD), BF) for j in range(nb)]
        scratch += [
            pltpu.VMEM((HEADS, Z, 2, rb, HD), BF),
            pltpu.VMEM((HEADS, Z, 2, rb, HD), BF),
            dma((2,)),
            dma((Z, 2)), dma((Z, 2)),
            dma((Z, 2, S)), dma((Z, 2, S)),
            dma((HEADS,)), dma((HEADS,)),
            dma((HEADS,)), dma((HEADS,)),
            dma((HEADS, 2, nb)), dma((HEADS, 2, nb)),
            dma((HEADS, Z)), dma((HEADS, Z)),
        ]
        return pl.pallas_call(
            functools.partial(kernel, N, Z, S, scale),
            out_shape=(
                jax.ShapeDtypeStruct((T, HW), BF),
                jax.ShapeDtypeStruct((T, D), BF),
                jax.ShapeDtypeStruct((T, HW), BF),
                jax.ShapeDtypeStruct((rb, 2 * HW), F32),
            ),
            in_specs=[vm] * 4,
            out_specs=(vm,) * 4,
            scratch_shapes=scratch,
            compiler_params=pltpu.CompilerParams(
                collective_id=0, has_side_effects=True, vmem_limit_bytes=58 * 1024 * 1024
            ),
            cost_estimate=pl.CostEstimate(flops=8 * T * D * HW * 2, bytes_accessed=8 * T * D, transcendentals=T * HW * 4),
        )(tokens, queries, kv_weight.reshape(S, r, 2 * HW), out_grad)

    spec = P(("dp", "seq"), None)
    return jax.shard_map(
        on_device, mesh=mesh, in_specs=(spec, spec, P("seq", None), spec),
        out_specs=(spec,) * 4, check_vma=False,
    )
```
